256 devices in a mesh: gx: 4 (over x), gy: 16 (over y_lo, z), gz: 4 (over y_hi, core).
Axes of the slice: x: 4, y: 4 (y_hi: 2, y_lo: 2; y = y_hi * 2 + y_lo), z: 8, core: 2. Of those that a mesh axis runs over, the one named last changes fastest.
Arguments:
- adjoint_now: float32 [160, 640, 512], P('gx', 'gy', 'gz'), may hold values from -6 to 6
- adjoint_late: float32 [160, 640, 512], P('gx', 'gy', 'gz'), may hold values from -6 to 6
- courant: float32 [160, 640, 512], P('gx', 'gy', 'gz'), may hold values from 0.05 to 0.18
- forward: bfloat16 [2, 160, 640, 512], P(None, 'gx', 'gy', 'gz'), may hold values from -6 to 6
- image_in: float32 [160, 640, 512], P('gx', 'gy', 'gz'), may hold values from -6 to 6
- traces: float32 [2, 65536], P(None, ('gy', 'gz')), may hold values from -6 to 6
- rec_owner: int32 [65536], P(('gy', 'gz')), may hold values from 0 to 255, as said below
- rec_cell: int32 [65536], P(('gy', 'gz')), may hold values from 0 to 204799, as said below
Outputs:
- adjoint_newest: float32 [160, 640, 512], P('gx', 'gy', 'gz')
- adjoint_middle: float32 [160, 640, 512], P('gx', 'gy', 'gz')
- image_out: float32 [160, 640, 512], P('gx', 'gy', 'gz')
The draws below stay inside these ranges and needn't reach their ends.
Inputs may be any that keep to these rules, and one draw needn't show every extreme that they name: `rec_owner`: the owner is the flat mesh index (gx * 16 + gy) * 4 + gz of the device whose block holds the receiver's cell, always with gz = 0. Among the records of one index of gy+gz at most 64 have one owner, and in every such block one owner has exactly 64. `rec_cell`: the cell within the owner's block, numbered (x * 40 + y) * 128 + z, with depth z below 8.
All inputs are finite; a program needn't handle non-finite values.
Results may differ from the reference program's by a relative error of at most 0.0003.
Values sent between devices are 32-bit elements; how exact they have to be, the bound alone decides.
No kernel may reach another device: no remote copies, remote signals or barrier semaphores. Data moves between devices by JAX's collectives and lax.ppermute only.
A program may use at most 128 MiB of HBM per device.

```python
import math
import jax
import jax.numpy as jnp
from jax import lax

CX = 40
CY = 40
CZ = 128
REC_DEV = 1024
STEPS = 2
SURF = 8
NX = 160
NY = 640
NZ = 512
GROUP = 64
OWNERS = 64
REC = 65536
CAP = 64
N_GY = 16
N_GZ = 4


def record_block(block_key):
    parts = jax.random.split(block_key, 7)
    full_owner = jax.random.randint(parts[0], (), 0, OWNERS, dtype=jnp.int32)
    others = jax.random.permutation(parts[1], OWNERS - 1).astype(jnp.int32)
    rest_count = REC_DEV - CAP
    index = jnp.arange(rest_count, dtype=jnp.int32)
    base = index * (OWNERS - 1) // rest_count
    label = (base + jax.random.randint(parts[2], (rest_count,), 0, 2, dtype=jnp.int32)) % (OWNERS - 1)
    chosen = others[label]
    chosen = chosen + (chosen >= full_owner).astype(jnp.int32)
    surface = jnp.concatenate([jnp.full((CAP,), full_owner, jnp.int32), chosen])
    surface = surface[jax.random.permutation(parts[3], REC_DEV)]
    owner = surface * N_GZ
    coord_x = jax.random.randint(parts[4], (REC_DEV,), 0, CX, dtype=jnp.int32)
    coord_y = jax.random.randint(parts[5], (REC_DEV,), 0, CY, dtype=jnp.int32)
    coord_z = jax.random.randint(parts[6], (REC_DEV,), 0, SURF, dtype=jnp.int32)
    return (owner, (coord_x * CY + coord_y) * CZ + coord_z)


def draw_records(key):
    block_keys = jax.random.split(jax.random.fold_in(key, 17), GROUP)
    owners, cellular = jax.vmap(record_block)(block_keys)
    return (owners.reshape(-1), cellular.reshape(-1))


def draw_rec_owner(key, part):
    return draw_records(key)[0]


def draw_rec_cell(key, part):
    return draw_records(key)[1]


def level_of(key, dims, shards, low, top_value):
    def one(axis_at, blocks):
        steps = jax.random.uniform(jax.random.fold_in(jax.random.fold_in(key, 6), axis_at), (blocks,), jnp.float32, low / len(shards), top_value / len(shards))
        return jnp.repeat(jnp.exp(steps), dims[axis_at] // blocks).reshape((-1,) + (1,) * (len(dims) - axis_at - 1))

    factor_of = one(*shards[0])
    for cut in shards[1:]:
        factor_of = factor_of * one(*cut)
    return factor_of


def noise(stream_key, extent, scale, limit, cuts=(), held_as=jnp.bfloat16):
    gain = level_of(stream_key, extent, cuts, -0.22, 0.18) if cuts else 1.0
    values = jax.random.normal(stream_key, extent, jnp.float32) * scale * gain
    return jnp.minimum(jnp.maximum(values, -limit), limit).astype(held_as)


def setup_inputs(seed: int = 0) -> dict:
    key_list = jax.random.split(jax.random.key(seed), 9)
    return {
        "adjoint_now": noise(key_list[0], (NX, NY, NZ), 1.0, 6.0, ((0, 4), (1, 16), (2, 4)), jnp.float32),
        "adjoint_late": noise(key_list[1], (NX, NY, NZ), 1.0, 6.0, ((0, 4), (1, 16), (2, 4)), jnp.float32),
        "courant": jnp.clip(jnp.exp(math.log(0.18) - 1.2809339 * jax.random.uniform(key_list[2], (NX, NY, NZ), jnp.float32) ** level_of(key_list[2], (NX, NY, NZ), ((0, 4), (1, 16), (2, 4)), -0.2, 0.2)), 0.05, 0.18),
        "forward": noise(key_list[3], (STEPS, NX, NY, NZ), 1.0, 6.0, ((1, 4), (2, 16), (3, 4))),
        "image_in": noise(key_list[4], (NX, NY, NZ), 1.0, 6.0, ((0, 4), (1, 16), (2, 4)), jnp.float32),
        "traces": noise(key_list[5], (STEPS, REC), 1.0, 6.0, ((1, 64),), jnp.float32),
        "rec_owner": draw_rec_owner(jax.random.fold_in(key_list[8], 71), 0),
        "rec_cell": draw_rec_cell(jax.random.fold_in(key_list[8], 71), 0),
    }


COEFFS = (-205.0 / 72.0, 8.0 / 5.0, -1.0 / 5.0, 8.0 / 315.0, -1.0 / 560.0)


def axis_part(field, axis):
    length = field.shape[axis]
    widths = [(0, 0), (0, 0), (0, 0)]
    widths[axis] = (4, 4)
    padded = jnp.pad(field, widths)
    summed = COEFFS[0] * field
    for shift in range(1, 5):
        upper = lax.slice_in_dim(padded, 4 + shift, 4 + shift + length, axis=axis)
        lower = lax.slice_in_dim(padded, 4 - shift, 4 - shift + length, axis=axis)
        summed = summed + COEFFS[shift] * (upper + lower)
    return summed


def laplacian(field):
    return axis_part(field, 0) + axis_part(field, 1) + axis_part(field, 2)


def reference(adjoint_now, adjoint_late, courant, forward, image_in, traces, rec_owner, rec_cell):
    block_x = rec_owner // (N_GY * N_GZ)
    block_y = (rec_owner // N_GZ) % N_GY
    block_z = rec_owner % N_GZ
    local_x = rec_cell // (CY * CZ)
    local_y = (rec_cell // CZ) % CY
    local_z = rec_cell % CZ
    global_cell = ((block_x * CX + local_x) * NY + block_y * CY + local_y) * NZ + block_z * CZ + local_z
    global_cell = global_cell.astype(jnp.int32)
    now = adjoint_now
    late = adjoint_late
    image = image_in
    for step in range(STEPS):
        sources = jnp.zeros((NX * NY * NZ,), jnp.float32).at[global_cell].add(traces[step])
        sources = sources.reshape(NX, NY, NZ)
        fresh = 2.0 * now - late + courant * (laplacian(now) + sources)
        image = image + forward[step].astype(jnp.float32) * fresh
        late = now
        now = fresh
    return now, late, image
```

```python
import functools

import jax
import jax.numpy as jnp
from jax import lax
from jax.experimental import pallas as pl
from jax.experimental.pallas import tpu as pltpu
from jax.sharding import PartitionSpec as P

COEFFS = (-205.0 / 72.0, 8.0 / 5.0, -1.0 / 5.0, 8.0 / 315.0, -1.0 / 560.0)
SURF = 8
CAP = 64
F32 = jnp.float32
BF16 = jnp.bfloat16
NT = (((1,), (1,)), ((), ()))
TN = (((0,), (0,)), ((), ()))


def split3(value):
    high = value.astype(BF16).astype(F32)
    rest = value - high
    middle = rest.astype(BF16).astype(F32)
    return high, middle, rest - middle


def iota(shape, dim):
    return lax.broadcasted_iota(jnp.int32, shape, dim)


def pack_kernel(n_gx, n_gy, n_gz, traces_ref, owner_ref, cell_ref, out_ref):
    me = lax.axis_index("gx")
    chunks = owner_ref.shape[0]
    owner_ids = iota((n_gy, 128), 0)
    picks = []
    for c in range(chunks):
        owner = owner_ref[c : c + 1, :]
        local = owner - me * (n_gy * n_gz)
        dest = lax.shift_right_arithmetic(local, n_gz.bit_length() - 1)
        picks.append(jnp.where(owner_ids == dest, 1.0, 0.0).astype(F32))
    all_picks = jnp.concatenate(picks, axis=0)
    before = (iota((128, 128), 0) < iota((128, 128), 1)).astype(F32).astype(BF16)
    prefix = jnp.dot(all_picks.astype(BF16), before, preferred_element_type=F32)
    offset = jnp.zeros((n_gy, 1), F32)
    slot_ids = iota((128, 128), 0)
    slots_low, slots_high, left, right = [], [], [], []
    for c in range(chunks):
        pick = picks[c]
        rank = jnp.sum(pick * (prefix[c * n_gy : (c + 1) * n_gy] + offset), axis=0, keepdims=True)
        offset = offset + jnp.sum(pick, axis=1, keepdims=True)
        rank = rank.astype(jnp.int32)
        slots_low.append(jnp.where(slot_ids == rank, 1.0, 0.0).astype(BF16))
        slots_high.append(jnp.where(slot_ids == rank + CAP, 1.0, 0.0).astype(BF16))
        first = traces_ref[0:1, c * 128 : (c + 1) * 128]
        second = traces_ref[1:2, c * 128 : (c + 1) * 128]
        cell = cell_ref[c : c + 1, :].astype(F32)
        left.append(
            jnp.concatenate([pick * s for s in split3(first) + split3(cell)], axis=0).astype(BF16)
        )
        right.append(jnp.concatenate([pick * s for s in split3(second)], axis=0).astype(BF16))
    low = jnp.concatenate(slots_low, axis=1)
    high = jnp.concatenate(slots_high, axis=1)
    left = lax.dot_general(jnp.concatenate(left, axis=1), low, NT, preferred_element_type=F32)
    right = lax.dot_general(jnp.concatenate(right, axis=1), high, NT, preferred_element_type=F32)

    def joined(value, at):
        parts = [value[(at + i) * n_gy : (at + i + 1) * n_gy] for i in range(3)]
        return parts[0] + parts[1] + parts[2]

    values = joined(left, 0) + joined(right, 0)
    cells = joined(left, 3)
    out_ref[...] = jnp.zeros_like(out_ref)
    for d in range(n_gy):
        out_ref[d, 0:1, :] = values[d : d + 1, :]
        out_ref[d, 1:2, :] = cells[d : d + 1, :]


def store_faces(read, cx, cy, xlo_ref, xhi_ref, ylo_ref, yhi_ref):
    half = cx // 2
    for i in range(4):
        xlo_ref[i] = read(i)
        xhi_ref[i] = read(cx - 4 + i)
    for x in range(half):
        one, two = read(x), read(x + half)
        ylo_ref[x] = jnp.concatenate([one[0:4], two[0:4]], axis=0)
        yhi_ref[x] = jnp.concatenate([one[cy - 4 : cy], two[cy - 4 : cy]], axis=0)


def depth_faces(value):
    rows = value.shape[0]
    at = iota((8, 128), 0)
    take = iota((8, 128), 1) == jnp.where(at < 4, at, at + 120)
    take = jnp.where(take, 1.0, 0.0).astype(BF16)
    parts = [
        lax.dot_general(take, s.astype(BF16), NT, preferred_element_type=F32) for s in split3(value)
    ]
    return parts[0] + parts[1] + parts[2]


def faces_kernel(now_ref, xlo_ref, xhi_ref, ylo_ref, yhi_ref, z_ref):
    cx, cy, cz = now_ref.shape
    store_faces(lambda x: now_ref[x], cx, cy, xlo_ref, xhi_ref, ylo_ref, yhi_ref)
    z_ref[...] = depth_faces(now_ref[...].reshape(cx * cy, cz))


def bin_records(recv_ref, cx, cy, cz):
    senders = recv_ref.shape[0]
    half = senders // 2
    values = recv_ref[:, 0, :]
    cells = recv_ref[:, 1, :]
    low = iota((half, 128), 1) < CAP
    rolled = pltpu.roll(values, CAP, 1)
    first = jnp.where(low, values[:half], rolled[half:])
    second = jnp.where(low, rolled[:half], values[half:])
    cell = jnp.where(low, cells[:half], pltpu.roll(cells, CAP, 1)[half:]).astype(jnp.int32)
    depth = lax.bitwise_and(cell, cz - 1)
    plane = lax.shift_right_logical(cell, cz.bit_length() - 1)
    at_x = plane // cy
    at_y = plane - at_x * cy
    column = at_x * SURF + depth
    columns = -(-cx * SURF // 128) * 128
    pieces = split3(first) + split3(second)
    row_ids = iota((cy, 128), 0)
    column_ids = iota((columns, 128), 0)
    total = None
    step = 4
    for begin in range(0, half, step):
        lefts, rights = [], []
        for s in range(begin, begin + step):
            hit = row_ids == at_y[s : s + 1]
            lefts.append(
                jnp.concatenate([jnp.where(hit, p[s : s + 1], 0.0) for p in pieces], axis=0).astype(BF16)
            )
            rights.append(jnp.where(column_ids == column[s : s + 1], 1.0, 0.0).astype(BF16))
        term = lax.dot_general(
            jnp.concatenate(lefts, axis=1), jnp.concatenate(rights, axis=1), NT,
            preferred_element_type=F32,
        )
        total = term if total is None else total + term
    part = [total[i * cy : (i + 1) * cy] for i in range(6)]
    return part[0] + part[1] + part[2], part[3] + part[4] + part[5]


def fill_padded(pad_ref, now_ref, xb_ref, xa_ref, yb_ref, ya_ref):
    cx, cy, cz = now_ref.shape
    half = cx // 2
    pad_ref[4 : 4 + cx, 8 : 8 + cy, :] = now_ref[...]
    pad_ref[0:4, 8 : 8 + cy, :] = xb_ref[...]
    pad_ref[4 + cx : 8 + cx, 8 : 8 + cy, :] = xa_ref[...]
    pad_ref[4 : 4 + half, 4:8, :] = yb_ref[:, 0:4, :]
    pad_ref[4 + half : 4 + cx, 4:8, :] = yb_ref[:, 4:8, :]
    pad_ref[4 : 4 + half, 8 + cy : 12 + cy, :] = ya_ref[:, 0:4, :]
    pad_ref[4 + half : 4 + cx, 8 + cy : 12 + cy, :] = ya_ref[:, 4:8, :]


def depth_correction(own, below, above):
    at = iota(own.shape, 0)
    delta = jnp.where(at < 4, above, below) - own
    row = iota((8, 128), 0)
    lane = iota((8, 128), 1)
    distance = jnp.where(row < 4, 128 + row - lane, lane + 8 - row)
    weight = jnp.zeros((8, 128), F32)
    for j in range(1, 5):
        weight = jnp.where(distance == j, COEFFS[j], weight)
    return lax.dot_general(
        delta, weight, TN, precision=lax.Precision.HIGHEST, preferred_element_type=F32
    )


def lap_at(pad_ref, zc_ref, x, cy):
    center = pad_ref[x + 4, 8 : 8 + cy, :]
    total = (3.0 * COEFFS[0]) * center + zc_ref[x]
    for j in range(1, 5):
        pair = pad_ref[x + 4 - j, 8 : 8 + cy, :] + pad_ref[x + 4 + j, 8 : 8 + cy, :]
        pair = pair + (pad_ref[x + 4, 8 - j : 8 - j + cy, :] + pad_ref[x + 4, 8 + j : 8 + j + cy, :])
        pair = pair + (pltpu.roll(center, j, 1) + pltpu.roll(center, 128 - j, 1))
        total = total + COEFFS[j] * pair
    return center, total


def source_at(sources, x, low):
    group, shift = x // 16, (x % 16) * SURF
    piece = sources[:, group * 128 : (group + 1) * 128]
    if shift:
        piece = pltpu.roll(piece, 128 - shift, 1)
    return jnp.where(low, piece, 0.0)


def first_kernel(
    recv_ref, now_ref, late_ref, courant_ref, forward_ref, image_ref,
    xb_ref, xa_ref, yb_ref, ya_ref, z_ref, zb_ref, za_ref,
    fresh_ref, image_out_ref, source_ref, xlo_ref, xhi_ref, ylo_ref, yhi_ref, zf_ref,
    pad_ref, zc_ref,
):
    cx, cy, cz = now_ref.shape
    fill_padded(pad_ref, now_ref, xb_ref, xa_ref, yb_ref, ya_ref)
    zc_ref[...] = depth_correction(z_ref[...], zb_ref[...], za_ref[...]).reshape(cx, cy, cz)
    sources, later = bin_records(recv_ref, cx, cy, cz)
    source_ref[...] = later
    low = iota((cy, cz), 1) < SURF
    for x in range(cx):
        center, lap = lap_at(pad_ref, zc_ref, x, cy)
        lap = lap + source_at(sources, x, low)
        fresh = 2.0 * center - late_ref[x] + courant_ref[x] * lap
        fresh_ref[x] = fresh
        image_out_ref[x] = image_ref[x] + forward_ref[0, x].astype(F32) * fresh
    store_faces(lambda x: fresh_ref[x], cx, cy, xlo_ref, xhi_ref, ylo_ref, yhi_ref)
    zf_ref[...] = depth_faces(fresh_ref[...].reshape(cx * cy, cz))


def second_kernel(
    now_ref, late_ref, courant_ref, forward_ref, image_ref, source_ref,
    xb_ref, xa_ref, yb_ref, ya_ref, z_ref, zb_ref, za_ref,
    fresh_ref, image_out_ref,
    pad_ref, zc_ref,
):
    cx, cy, cz = now_ref.shape
    fill_padded(pad_ref, now_ref, xb_ref, xa_ref, yb_ref, ya_ref)
    zc_ref[...] = depth_correction(z_ref[...], zb_ref[...], za_ref[...]).reshape(cx, cy, cz)
    sources = source_ref[...]
    low = iota((cy, cz), 1) < SURF
    for x in range(cx):
        center, lap = lap_at(pad_ref, zc_ref, x, cy)
        lap = lap + source_at(sources, x, low)
        fresh = 2.0 * center - late_ref[x] + courant_ref[x] * lap
        fresh_ref[x] = fresh
        image_out_ref[x] = image_ref[x] + forward_ref[1, x].astype(F32) * fresh


def shift(value, axis, by):
    count = lax.axis_size(axis)
    pairs = [(i, i + by) for i in range(count) if 0 <= i + by < count]
    return lax.ppermute(value, axis, pairs)


def exchange(faces):
    xlo, xhi, ylo, yhi, z = faces
    yb, ya = shift(yhi, "gy", 1), shift(ylo, "gy", -1)
    xb, xa = shift(xhi, "gx", 1), shift(xlo, "gx", -1)
    zb, za = shift(z, "gz", 1), shift(z, "gz", -1)
    return xb, xa, yb, ya, z, zb, za


def struct(*shape):
    return jax.ShapeDtypeStruct(shape, F32)


def call(kernel, outs, flops, args, scratch=()):
    vmem = pl.BlockSpec(memory_space=pltpu.VMEM)
    size = sum(a.size * a.dtype.itemsize for a in args) + sum(o.size * 4 for o in outs)
    return pl.pallas_call(
        kernel,
        out_shape=outs,
        in_specs=[vmem] * len(args),
        out_specs=[vmem] * len(outs),
        scratch_shapes=list(scratch),
        compiler_params=pltpu.CompilerParams(vmem_limit_bytes=40 * 2**20),
        cost_estimate=pl.CostEstimate(flops=flops, bytes_accessed=size, transcendentals=0),
    )(*args)


def on_device(adjoint_now, adjoint_late, courant, forward, image_in, traces, rec_owner, rec_cell):
    cx, cy, cz = adjoint_now.shape
    n_gx, n_gy, n_gz = (lax.axis_size(a) for a in ("gx", "gy", "gz"))
    chunks = rec_owner.shape[0] // 128
    block = struct(cx, cy, cz)
    faces = (
        struct(4, cy, cz), struct(4, cy, cz),
        struct(cx // 2, 8, cz), struct(cx // 2, 8, cz), struct(8, cx * cy),
    )
    (packed,) = call(
        functools.partial(pack_kernel, n_gx, n_gy, n_gz),
        (struct(n_gy * n_gz, 2, 128),), 10**7,
        (traces, rec_owner.reshape(chunks, 128), rec_cell.reshape(chunks, 128)),
    )
    received = lax.all_to_all(packed, ("gz", "gy"), 0, 0)
    halo = exchange(call(faces_kernel, faces, 10**7, (adjoint_now,)))
    scratch = (pltpu.VMEM((cx + 8, cy + 16, cz), F32), pltpu.VMEM((cx, cy, cz), F32))
    columns = -(-cx * SURF // 128) * 128
    middle, image, later, *out_faces = call(
        first_kernel, (block, block, struct(cy, columns)) + faces, 10**8,
        (received, adjoint_now, adjoint_late, courant, forward, image_in) + halo, scratch,
    )
    halo = exchange(out_faces)
    newest, image = call(
        second_kernel, (block, block), 10**8,
        (middle, adjoint_now, courant, forward, image, later) + halo, scratch,
    )
    return newest, middle, image


def solution(mesh):
    grid = P("gx", "gy", "gz")
    return jax.shard_map(
        on_device,
        mesh=mesh,
        in_specs=(
            grid, grid, grid, P(None, "gx", "gy", "gz"), grid,
            P(None, ("gy", "gz")), P(("gy", "gz")), P(("gy", "gz")),
        ),
        out_specs=(grid, grid, grid),
        check_vma=False,
    )
```

```python
import functools

import jax
import jax.numpy as jnp
from jax import lax
from jax.experimental import pallas as pl
from jax.experimental.pallas import tpu as pltpu
from jax.sharding import PartitionSpec as P

COEFFS = (-205.0 / 72.0, 8.0 / 5.0, -1.0 / 5.0, 8.0 / 315.0, -1.0 / 560.0)
SURF = 8
CAP = 64
CHUNK = 20
UNROLL = 20
F32 = jnp.float32
BF16 = jnp.bfloat16
NT = (((1,), (1,)), ((), ()))
TN = (((0,), (0,)), ((), ()))


def split3(value):
    high = value.astype(BF16).astype(F32)
    rest = value - high
    middle = rest.astype(BF16).astype(F32)
    return high, middle, rest - middle


def iota(shape, dim):
    return lax.broadcasted_iota(jnp.int32, shape, dim)


def pack_records(n_gy, n_gz, traces_ref, owner_ref, cell_ref, out_ref):
    me = lax.axis_index("gx")
    chunks = owner_ref.shape[0]
    owner_ids = iota((n_gy, 128), 0)
    picks = []
    for c in range(chunks):
        owner = owner_ref[c : c + 1, :]
        local = owner - me * (n_gy * n_gz)
        dest = lax.shift_right_arithmetic(local, n_gz.bit_length() - 1)
        picks.append(jnp.where(owner_ids == dest, 1.0, 0.0).astype(F32))
    all_picks = jnp.concatenate(picks, axis=0)
    before = (iota((128, 128), 0) < iota((128, 128), 1)).astype(F32).astype(BF16)
    prefix = jnp.dot(all_picks.astype(BF16), before, preferred_element_type=F32)
    offset = jnp.zeros((n_gy, 1), F32)
    slot_ids = iota((128, 128), 0)
    slots_low, slots_high, left, right = [], [], [], []
    for c in range(chunks):
        pick = picks[c]
        rank = jnp.sum(pick * (prefix[c * n_gy : (c + 1) * n_gy] + offset), axis=0, keepdims=True)
        offset = offset + jnp.sum(pick, axis=1, keepdims=True)
        rank = rank.astype(jnp.int32)
        slots_low.append(jnp.where(slot_ids == rank, 1.0, 0.0).astype(BF16))
        slots_high.append(jnp.where(slot_ids == rank + CAP, 1.0, 0.0).astype(BF16))
        first = traces_ref[0:1, c * 128 : (c + 1) * 128]
        second = traces_ref[1:2, c * 128 : (c + 1) * 128]
        cell = cell_ref[c : c + 1, :].astype(F32)
        left.append(
            jnp.concatenate([pick * s for s in split3(first) + split3(cell)], axis=0).astype(BF16)
        )
        right.append(jnp.concatenate([pick * s for s in split3(second)], axis=0).astype(BF16))
    low = jnp.concatenate(slots_low, axis=1)
    high = jnp.concatenate(slots_high, axis=1)
    left = lax.dot_general(jnp.concatenate(left, axis=1), low, NT, preferred_element_type=F32)
    right = lax.dot_general(jnp.concatenate(right, axis=1), high, NT, preferred_element_type=F32)

    def joined(value, at):
        parts = [value[(at + i) * n_gy : (at + i + 1) * n_gy] for i in range(3)]
        return parts[0] + parts[1] + parts[2]

    values = joined(left, 0) + joined(right, 0)
    cells = joined(left, 3)
    out_ref[...] = jnp.zeros_like(out_ref)
    for d in range(n_gy):
        out_ref[d, 0:1, :] = values[d : d + 1, :]
        out_ref[d, 1:2, :] = cells[d : d + 1, :]


def is_even(axis):
    return lax.rem(lax.axis_index(axis), 2) == 0


def store_y_faces(read, half, cy, y0_ref, y1_ref, begin, end):
    y_even = is_even("gy")
    for x in range(begin, end):
        one, two = read(x), read(x + half)
        lo = jnp.concatenate([one[0:4], two[0:4]], axis=0)
        hi = jnp.concatenate([one[cy - 4 : cy], two[cy - 4 : cy]], axis=0)
        y0_ref[x] = jnp.where(y_even, hi, lo)
        y1_ref[x] = jnp.where(y_even, lo, hi)


def x_faces(ref):
    cx = ref.shape[0]
    first = jnp.where(is_even("gx"), cx - 4, 0)
    return ref.at[pl.ds(first, 4)], ref.at[pl.ds(cx - 4 - first, 4)]


class Copier:
    def __init__(self, sems):
        self.sems, self.used, self.open = sems, 0, []

    def start(self, src, dst):
        copy = pltpu.make_async_copy(src, dst, self.sems.at[self.used])
        self.used += 1
        copy.start()
        return copy

    def send(self, src, dst):
        self.open.append(self.start(src, dst))

    def close(self):
        for copy in self.open:
            copy.wait()


def depth_faces(value):
    at = iota((8, 128), 0)
    take = iota((8, 128), 1) == jnp.where(at < 4, at, at + 120)
    take = jnp.where(take, 1.0, 0.0).astype(BF16)
    parts = [
        lax.dot_general(take, s.astype(BF16), NT, preferred_element_type=F32) for s in split3(value)
    ]
    return parts[0] + parts[1] + parts[2]


def send_kernel(
    n_gy, n_gz, traces_hbm, owner_hbm, cell_hbm, now_hbm,
    packed_hbm, x0_hbm, x1_hbm, y0_hbm, y1_hbm, z_hbm,
    traces_ref, owner_ref, cell_ref, now_ref, packed_ref, y0_ref, y1_ref, z_ref, sems,
):
    cx, cy, cz = now_ref.shape
    copier = Copier(sems)
    pairs = ((traces_hbm, traces_ref), (owner_hbm, owner_ref), (cell_hbm, cell_ref))
    records = [copier.start(src, dst) for src, dst in pairs]
    now = copier.start(now_hbm, now_ref)
    for copy in records:
        copy.wait()
    pack_records(n_gy, n_gz, traces_ref, owner_ref, cell_ref, packed_ref)
    copier.send(packed_ref, packed_hbm)
    now.wait()
    for src, dst in zip(x_faces(now_ref), (x0_hbm, x1_hbm)):
        copier.send(src, dst)
    store_y_faces(lambda x: now_ref[x], cx // 2, cy, y0_ref, y1_ref, 0, cx // 2)
    copier.send(y0_ref, y0_hbm)
    copier.send(y1_ref, y1_hbm)
    z_ref[...] = depth_faces(now_ref[...].reshape(cx * cy, cz))
    copier.send(z_ref, z_hbm)
    copier.close()


def bin_records(recv_ref, cx, cy, cz):
    senders = recv_ref.shape[0]
    half = senders // 2
    values = recv_ref[:, 0, :]
    cells = recv_ref[:, 1, :]
    low = iota((half, 128), 1) < CAP
    rolled = pltpu.roll(values, CAP, 1)
    first = jnp.where(low, values[:half], rolled[half:])
    second = jnp.where(low, rolled[:half], values[half:])
    cell = jnp.where(low, cells[:half], pltpu.roll(cells, CAP, 1)[half:]).astype(jnp.int32)
    depth = lax.bitwise_and(cell, cz - 1)
    plane = lax.shift_right_logical(cell, cz.bit_length() - 1)
    at_x = plane // cy
    at_y = plane - at_x * cy
    column = at_x * SURF + depth
    columns = -(-cx * SURF // 128) * 128
    pieces = split3(first) + split3(second)
    row_ids = iota((cy, 128), 0)
    column_ids = iota((columns, 128), 0)
    total = None
    step = 4
    for begin in range(0, half, step):
        lefts, rights = [], []
        for s in range(begin, begin + step):
            hit = row_ids == at_y[s : s + 1]
            lefts.append(
                jnp.concatenate([jnp.where(hit, p[s : s + 1], 0.0) for p in pieces], axis=0).astype(BF16)
            )
            rights.append(jnp.where(column_ids == column[s : s + 1], 1.0, 0.0).astype(BF16))
        term = lax.dot_general(
            jnp.concatenate(lefts, axis=1), jnp.concatenate(rights, axis=1), NT,
            preferred_element_type=F32,
        )
        total = term if total is None else total + term
    part = [total[i * cy : (i + 1) * cy] for i in range(6)]
    return part[0] + part[1] + part[2], part[3] + part[4] + part[5]


def start_halo(copier, pad_ref, halo_hbm, halo_refs):
    cx, cy = pad_ref.shape[0] - 8, pad_ref.shape[1] - 16
    first = jnp.where(is_even("gx"), 4 + cx, 0)
    places = (
        pad_ref.at[pl.ds(first, 4), 8 : 8 + cy, :],
        pad_ref.at[pl.ds(4 + cx - first, 4), 8 : 8 + cy, :],
    ) + tuple(halo_refs)
    return [copier.start(src, dst) for src, dst in zip(halo_hbm, places)]


def fill_y(pad_ref, y0_ref, y1_ref):
    cx, cy = pad_ref.shape[0] - 8, pad_ref.shape[1] - 16
    half = cx // 2
    y_even = is_even("gy")
    for x in range(half):
        one, two = y0_ref[x], y1_ref[x]
        before, after = jnp.where(y_even, two, one), jnp.where(y_even, one, two)
        pad_ref[4 + x, 4:8, :] = before[0:4]
        pad_ref[4 + half + x, 4:8, :] = before[4:8]
        pad_ref[4 + x, 8 + cy : 12 + cy, :] = after[0:4]
        pad_ref[4 + half + x, 8 + cy : 12 + cy, :] = after[4:8]


def depth_correction(own, zero, one):
    upper = (iota(own.shape, 0) < 4) == is_even("gz")
    delta = jnp.where(upper, zero, one) - own
    row = iota((8, 128), 0)
    lane = iota((8, 128), 1)
    distance = jnp.where(row < 4, 128 + row - lane, lane + 8 - row)
    weight = jnp.zeros((8, 128), F32)
    for j in range(1, 5):
        weight = jnp.where(distance == j, COEFFS[j], weight)
    return lax.dot_general(
        delta, weight, TN, precision=lax.Precision.HIGHEST, preferred_element_type=F32
    )


def lap_at(pad_ref, zc_ref, x, cy):
    center = pad_ref[x + 4, 8 : 8 + cy, :]
    total = (3.0 * COEFFS[0]) * center + zc_ref[x]
    for j in range(1, 5):
        pair = pad_ref[x + 4 - j, 8 : 8 + cy, :] + pad_ref[x + 4 + j, 8 : 8 + cy, :]
        pair = pair + (pad_ref[x + 4, 8 - j : 8 - j + cy, :] + pad_ref[x + 4, 8 + j : 8 + j + cy, :])
        pair = pair + (pltpu.roll(center, j, 1) + pltpu.roll(center, 128 - j, 1))
        total = total + COEFFS[j] * pair
    return center, total


def spread_sources(sources, out_ref):
    for group in range(out_ref.shape[0]):
        out_ref[group] = sources[:, group * 128 : (group + 1) * 128]


def source_at(source_ref, x, low):
    piece = source_ref[x // 16]
    piece = pltpu.roll(piece, lax.rem(128 - lax.rem(x, 16) * SURF, 128), 1)
    return jnp.where(low, piece, 0.0)


def center_copy(copier, hbm, pad_ref):
    cx, cy = pad_ref.shape[0] - 8, pad_ref.shape[1] - 16
    return copier.start(hbm, pad_ref.at[4 : 4 + cx, 8 : 8 + cy, :])


def start_chunks(copier, pairs, cx):
    chunks = []
    for begin in range(0, cx, CHUNK):
        part = pl.ds(begin, CHUNK)
        chunks.append([copier.start(src.at[part], dst.at[part]) for src, dst in pairs])
    return chunks


def first_kernel(
    recv_hbm, x0_hbm, x1_hbm, y0_hbm, y1_hbm, z_hbm, z0_hbm, z1_hbm,
    now_hbm, late_hbm, courant_hbm,
    fresh_hbm, source_hbm, xs0_hbm, xs1_hbm, ys0_hbm, ys1_hbm, zs_hbm,
    recv_ref, pad_ref, y0_ref, y1_ref, z_ref, z0_ref, z1_ref, zc_ref, late_ref, courant_ref,
    fresh_ref, source_ref, later_ref, ys0_ref, ys1_ref, zs_ref, sems,
):
    cx, cy, cz = fresh_ref.shape
    copier = Copier(sems)
    recv = copier.start(recv_hbm, recv_ref)
    halo = start_halo(
        copier, pad_ref, (x0_hbm, x1_hbm, y0_hbm, y1_hbm, z_hbm, z0_hbm, z1_hbm),
        (y0_ref, y1_ref, z_ref, z0_ref, z1_ref),
    )
    now = center_copy(copier, now_hbm, pad_ref)
    chunks = start_chunks(copier, ((late_hbm, late_ref), (courant_hbm, courant_ref)), cx)
    recv.wait()
    sources, later = bin_records(recv_ref, cx, cy, cz)
    spread_sources(sources, source_ref)
    spread_sources(later, later_ref)
    copier.send(later_ref, source_hbm)
    for copy in halo:
        copy.wait()
    fill_y(pad_ref, y0_ref, y1_ref)
    zc_ref[...] = depth_correction(z_ref[...], z0_ref[...], z1_ref[...]).reshape(cx, cy, cz)
    now.wait()
    low = iota((cy, cz), 1) < SURF

    def body(x, carry):
        center, lap = lap_at(pad_ref, zc_ref, x, cy)
        lap = lap + source_at(source_ref, x, low)
        fresh_ref[x] = 2.0 * center - late_ref[x] + courant_ref[x] * lap
        return carry

    for c, copies in enumerate(chunks):
        for copy in copies:
            copy.wait()
        part = pl.ds(c * CHUNK, CHUNK)
        lax.fori_loop(c * CHUNK, (c + 1) * CHUNK, body, 0, unroll=UNROLL)
        copier.send(fresh_ref.at[part], fresh_hbm.at[part])
    for src, dst in zip(x_faces(fresh_ref), (xs0_hbm, xs1_hbm)):
        copier.send(src, dst)
    store_y_faces(lambda x: fresh_ref[x], cx // 2, cy, ys0_ref, ys1_ref, 0, cx // 2)
    copier.send(ys0_ref, ys0_hbm)
    copier.send(ys1_ref, ys1_hbm)
    zs_ref[...] = depth_faces(fresh_ref[...].reshape(cx * cy, cz))
    copier.send(zs_ref, zs_hbm)
    copier.close()


def second_kernel(
    now_hbm, source_hbm, x0_hbm, x1_hbm, y0_hbm, y1_hbm, z_hbm, z0_hbm, z1_hbm,
    late_hbm, courant_hbm, forward_hbm, image_hbm,
    fresh_hbm, image_out_hbm,
    source_ref, pad_ref, y0_ref, y1_ref, z_ref, z0_ref, z1_ref, zc_ref, late_ref, courant_ref,
    forward0_ref, forward1_ref, image_ref, fresh_ref, sems,
):
    cx, cy, cz = fresh_ref.shape
    copier = Copier(sems)
    halo = start_halo(
        copier, pad_ref, (x0_hbm, x1_hbm, y0_hbm, y1_hbm, z_hbm, z0_hbm, z1_hbm),
        (y0_ref, y1_ref, z_ref, z0_ref, z1_ref),
    )
    now = center_copy(copier, now_hbm, pad_ref)
    source = copier.start(source_hbm, source_ref)
    chunks = start_chunks(
        copier,
        (
            (late_hbm, late_ref), (courant_hbm, courant_ref), (image_hbm, image_ref),
            (forward_hbm.at[0], forward0_ref), (forward_hbm.at[1], forward1_ref),
        ),
        cx,
    )
    for copy in halo:
        copy.wait()
    fill_y(pad_ref, y0_ref, y1_ref)
    zc_ref[...] = depth_correction(z_ref[...], z0_ref[...], z1_ref[...]).reshape(cx, cy, cz)
    now.wait()
    source.wait()
    low = iota((cy, cz), 1) < SURF

    def body(x, carry):
        center, lap = lap_at(pad_ref, zc_ref, x, cy)
        lap = lap + source_at(source_ref, x, low)
        fresh = 2.0 * center - late_ref[x] + courant_ref[x] * lap
        fresh_ref[x] = fresh
        image = image_ref[x] + forward0_ref[x].astype(F32) * center
        image_ref[x] = image + forward1_ref[x].astype(F32) * fresh
        return carry

    for c, copies in enumerate(chunks):
        for copy in copies:
            copy.wait()
        part = pl.ds(c * CHUNK, CHUNK)
        lax.fori_loop(c * CHUNK, (c + 1) * CHUNK, body, 0, unroll=UNROLL)
        copier.send(fresh_ref.at[part], fresh_hbm.at[part])
        copier.send(image_ref.at[part], image_out_hbm.at[part])
    copier.close()


def swap(value, axis, parity):
    pairs = []
    for i in range(parity, lax.axis_size(axis) - 1, 2):
        pairs += [(i, i + 1), (i + 1, i)]
    return lax.ppermute(value, axis, pairs)


def exchange(x0, x1, y0, y1, z):
    return (
        swap(x0, "gx", 0), swap(x1, "gx", 1),
        swap(y0, "gy", 0), swap(y1, "gy", 1),
        z, swap(z, "gz", 0), swap(z, "gz", 1),
    )


def struct(*shape):
    return jax.ShapeDtypeStruct(shape, F32)


def vm(*shape, dtype=F32):
    return pltpu.VMEM(shape, dtype)


def call(kernel, outs, args, scratch, copies):
    anywhere = pl.BlockSpec(memory_space=pl.ANY)
    size = sum(a.size * a.dtype.itemsize for a in args) + sum(o.size * 4 for o in outs)
    return pl.pallas_call(
        kernel,
        out_shape=outs,
        in_specs=[anywhere] * len(args),
        out_specs=[anywhere] * len(outs),
        scratch_shapes=list(scratch) + [pltpu.SemaphoreType.DMA((copies,))],
        compiler_params=pltpu.CompilerParams(vmem_limit_bytes=60 * 2**20),
        cost_estimate=pl.CostEstimate(flops=10**10, bytes_accessed=size, transcendentals=0),
    )(*args)


def on_device(adjoint_now, adjoint_late, courant, forward, image_in, traces, rec_owner, rec_cell):
    cx, cy, cz = adjoint_now.shape
    n_gy, n_gz = lax.axis_size("gy"), lax.axis_size("gz")
    chunks = rec_owner.shape[0] // 128
    groups = -(-cx * SURF // 128)
    block = struct(cx, cy, cz)
    x_face, y_face = struct(4, cy, cz), struct(cx // 2, 8, cz)
    faces = (x_face, x_face, y_face, y_face, struct(8, cx * cy))
    grid, y_in, z_in = vm(cx, cy, cz), vm(cx // 2, 8, cz), vm(8, cx * cy)
    pad = vm(cx + 8, cy + 16, cz)
    slots = (n_gy * n_gz, 2, 128)
    packed, *out_faces = call(
        functools.partial(send_kernel, n_gy, n_gz), (struct(*slots),) + faces,
        (traces, rec_owner.reshape(chunks, 128), rec_cell.reshape(chunks, 128), adjoint_now),
        (
            vm(*traces.shape), vm(chunks, 128, dtype=jnp.int32), vm(chunks, 128, dtype=jnp.int32),
            grid, vm(*slots), y_in, y_in, z_in,
        ),
        10,
    )
    received = lax.all_to_all(packed, ("gz", "gy"), 0, 0)
    halo = exchange(*out_faces)
    turns = cx // CHUNK
    source = (groups, cy, 128)
    middle, later, *out_faces = call(
        first_kernel, (block, struct(*source)) + faces,
        (received,) + halo + (adjoint_now, adjoint_late, courant),
        (
            vm(*slots), pad, y_in, y_in, z_in, z_in, z_in, grid, grid, grid,
            grid, vm(*source), vm(*source), y_in, y_in, z_in,
        ),
        15 + 3 * turns,
    )
    halo = exchange(*out_faces)
    half = vm(cx, cy, cz, dtype=BF16)
    newest, image = call(
        second_kernel, (block, block),
        (middle, later) + halo + (adjoint_now, courant, forward, image_in),
        (
            vm(*source), pad, y_in, y_in, z_in, z_in, z_in, grid, grid, grid,
            half, half, grid, grid,
        ),
        9 + 7 * turns,
    )
    return newest, middle, image


def solution(mesh):
    grid = P("gx", "gy", "gz")
    return jax.shard_map(
        on_device,
        mesh=mesh,
        in_specs=(
            grid, grid, grid, P(None, "gx", "gy", "gz"), grid,
            P(None, ("gy", "gz")), P(("gy", "gz")), P(("gy", "gz")),
        ),
        out_specs=(grid, grid, grid),
        check_vma=False,
    )
```

```python
import functools

import jax
import jax.numpy as jnp
from jax import lax
from jax.experimental import pallas as pl
from jax.experimental.pallas import tpu as pltpu
from jax.sharding import PartitionSpec as P

COEFFS = (-205.0 / 72.0, 8.0 / 5.0, -1.0 / 5.0, 8.0 / 315.0, -1.0 / 560.0)
SURF = 8
CAP = 64
CHUNK = 20
UNROLL = 20
F32 = jnp.float32
BF16 = jnp.bfloat16
NT = (((1,), (1,)), ((), ()))
TN = (((0,), (0,)), ((), ()))


def split3(value):
    high = value.astype(BF16).astype(F32)
    rest = value - high
    middle = rest.astype(BF16).astype(F32)
    return high, middle, rest - middle


def iota(shape, dim):
    return lax.broadcasted_iota(jnp.int32, shape, dim)


def pack_records(n_gy, n_gz, traces_ref, owner_ref, cell_ref, out_ref):
    me = lax.axis_index("gx")
    chunks = owner_ref.shape[0]
    owner_ids = iota((n_gy, 128), 0)
    picks = []
    for c in range(chunks):
        owner = owner_ref[c : c + 1, :]
        local = owner - me * (n_gy * n_gz)
        dest = lax.shift_right_arithmetic(local, n_gz.bit_length() - 1)
        picks.append(jnp.where(owner_ids == dest, 1.0, 0.0).astype(F32))
    all_picks = jnp.concatenate(picks, axis=0)
    before = (iota((128, 128), 0) < iota((128, 128), 1)).astype(F32).astype(BF16)
    prefix = jnp.dot(all_picks.astype(BF16), before, preferred_element_type=F32)
    offset = jnp.zeros((n_gy, 1), F32)
    slot_ids = iota((128, 128), 0)
    slots_low, slots_high, left, right = [], [], [], []
    for c in range(chunks):
        pick = picks[c]
        rank = jnp.sum(pick * (prefix[c * n_gy : (c + 1) * n_gy] + offset), axis=0, keepdims=True)
        offset = offset + jnp.sum(pick, axis=1, keepdims=True)
        rank = rank.astype(jnp.int32)
        slots_low.append(jnp.where(slot_ids == rank, 1.0, 0.0).astype(BF16))
        slots_high.append(jnp.where(slot_ids == rank + CAP, 1.0, 0.0).astype(BF16))
        first = traces_ref[0:1, c * 128 : (c + 1) * 128]
        second = traces_ref[1:2, c * 128 : (c + 1) * 128]
        cell = cell_ref[c : c + 1, :].astype(F32)
        left.append(
            jnp.concatenate([pick * s for s in split3(first) + split3(cell)], axis=0).astype(BF16)
        )
        right.append(jnp.concatenate([pick * s for s in split3(second)], axis=0).astype(BF16))
    low = jnp.concatenate(slots_low, axis=1)
    high = jnp.concatenate(slots_high, axis=1)
    left = lax.dot_general(jnp.concatenate(left, axis=1), low, NT, preferred_element_type=F32)
    right = lax.dot_general(jnp.concatenate(right, axis=1), high, NT, preferred_element_type=F32)

    def joined(value, at):
        parts = [value[(at + i) * n_gy : (at + i + 1) * n_gy] for i in range(3)]
        return parts[0] + parts[1] + parts[2]

    values = joined(left, 0) + joined(right, 0)
    cells = joined(left, 3)
    out_ref[...] = jnp.zeros_like(out_ref)
    for d in range(n_gy):
        out_ref[d, 0:1, :] = values[d : d + 1, :]
        out_ref[d, 1:2, :] = cells[d : d + 1, :]


def store_y_faces(src_ref, low_ref, high_ref):
    cx, cy, _ = src_ref.shape
    half = cx // 2
    for x in range(half):
        one, two = src_ref[x], src_ref[x + half]
        low_ref[x] = jnp.concatenate([one[0:4], two[0:4]], axis=0)
        high_ref[x] = jnp.concatenate([one[cy - 4 : cy], two[cy - 4 : cy]], axis=0)


def x_faces(ref):
    cx = ref.shape[0]
    return ref.at[0:4], ref.at[cx - 4 : cx]


def at_edges(axis):
    at = lax.axis_index(axis)
    return at == 0, at == lax.axis_size(axis) - 1


class Copier:
    def __init__(self, sems):
        self.sems, self.used, self.open = sems, 0, []

    def start(self, src, dst):
        copy = pltpu.make_async_copy(src, dst, self.sems.at[self.used])
        self.used += 1
        copy.start()
        return copy

    def send(self, src, dst):
        self.open.append(self.start(src, dst))

    def close(self):
        for copy in self.open:
            copy.wait()


def depth_faces(value):
    at = iota((8, 128), 0)
    take = iota((8, 128), 1) == jnp.where(at < 4, at, at + 120)
    take = jnp.where(take, 1.0, 0.0).astype(BF16)
    parts = [
        lax.dot_general(take, s.astype(BF16), NT, preferred_element_type=F32) for s in split3(value)
    ]
    return parts[0] + parts[1] + parts[2]


def send_kernel(
    n_gy, n_gz, traces_hbm, owner_hbm, cell_hbm, now_hbm,
    packed_hbm, x0_hbm, x1_hbm, y0_hbm, y1_hbm, z_hbm,
    traces_ref, owner_ref, cell_ref, now_ref, packed_ref, y0_ref, y1_ref, z_ref, sems,
):
    cx, cy, cz = now_ref.shape
    copier = Copier(sems)
    pairs = ((traces_hbm, traces_ref), (owner_hbm, owner_ref), (cell_hbm, cell_ref))
    records = [copier.start(src, dst) for src, dst in pairs]
    now = copier.start(now_hbm, now_ref)
    for copy in records:
        copy.wait()
    pack_records(n_gy, n_gz, traces_ref, owner_ref, cell_ref, packed_ref)
    copier.send(packed_ref, packed_hbm)
    now.wait()
    for src, dst in zip(x_faces(now_ref), (x0_hbm, x1_hbm)):
        copier.send(src, dst)
    store_y_faces(now_ref, y0_ref, y1_ref)
    copier.send(y0_ref, y0_hbm)
    copier.send(y1_ref, y1_hbm)
    z_ref[...] = depth_faces(now_ref[...].reshape(cx * cy, cz))
    copier.send(z_ref, z_hbm)
    copier.close()


def bin_records(recv_ref, cx, cy, cz):
    senders = recv_ref.shape[0]
    half = senders // 2
    values = recv_ref[:, 0, :]
    cells = recv_ref[:, 1, :]
    low = iota((half, 128), 1) < CAP
    rolled = pltpu.roll(values, CAP, 1)
    first = jnp.where(low, values[:half], rolled[half:])
    second = jnp.where(low, rolled[:half], values[half:])
    cell = jnp.where(low, cells[:half], pltpu.roll(cells, CAP, 1)[half:]).astype(jnp.int32)
    depth = lax.bitwise_and(cell, cz - 1)
    plane = lax.shift_right_logical(cell, cz.bit_length() - 1)
    at_x = plane // cy
    at_y = plane - at_x * cy
    column = at_x * SURF + depth
    columns = -(-cx * SURF // 128) * 128
    pieces = split3(first) + split3(second)
    row_ids = iota((cy, 128), 0)
    column_ids = iota((columns, 128), 0)
    total = None
    step = 4
    for begin in range(0, half, step):
        lefts, rights = [], []
        for s in range(begin, begin + step):
            hit = row_ids == at_y[s : s + 1]
            lefts.append(
                jnp.concatenate([jnp.where(hit, p[s : s + 1], 0.0) for p in pieces], axis=0).astype(BF16)
            )
            rights.append(jnp.where(column_ids == column[s : s + 1], 1.0, 0.0).astype(BF16))
        term = lax.dot_general(
            jnp.concatenate(lefts, axis=1), jnp.concatenate(rights, axis=1), NT,
            preferred_element_type=F32,
        )
        total = term if total is None else total + term
    part = [total[i * cy : (i + 1) * cy] for i in range(6)]
    return part[0] + part[1] + part[2], part[3] + part[4] + part[5]


def start_halo(copier, pad_ref, halo_hbm, halo_refs):
    cx, cy = pad_ref.shape[0] - 8, pad_ref.shape[1] - 16
    places = (pad_ref.at[0:4, 8 : 8 + cy, :], pad_ref.at[4 + cx : 8 + cx, 8 : 8 + cy, :])
    return [copier.start(src, dst) for src, dst in zip(halo_hbm, places + tuple(halo_refs))]


def fill_xy(pad_ref, before_ref, after_ref):
    cx, cy, cz = pad_ref.shape[0] - 8, pad_ref.shape[1] - 16, pad_ref.shape[2]
    half = cx // 2
    for edge, begin in zip(at_edges("gx"), (0, 4 + cx)):

        @pl.when(edge)
        def _(begin=begin):
            pad_ref[begin : begin + 4, 8 : 8 + cy, :] = jnp.zeros((4, cy, cz), F32)

    first, last = at_edges("gy")
    for x in range(half):
        before = jnp.where(first, 0.0, before_ref[x])
        after = jnp.where(last, 0.0, after_ref[x])
        pad_ref[4 + x, 4:8, :] = before[0:4]
        pad_ref[4 + half + x, 4:8, :] = before[4:8]
        pad_ref[4 + x, 8 + cy : 12 + cy, :] = after[0:4]
        pad_ref[4 + half + x, 8 + cy : 12 + cy, :] = after[4:8]


def depth_correction(own, before, after):
    at = iota(own.shape, 0)
    first, last = at_edges("gz")
    delta = jnp.where(at < 4, jnp.where(last, 0.0, after), jnp.where(first, 0.0, before)) - own
    row = iota((8, 128), 0)
    lane = iota((8, 128), 1)
    distance = jnp.where(row < 4, 128 + row - lane, lane + 8 - row)
    weight = jnp.zeros((8, 128), F32)
    for j in range(1, 5):
        weight = jnp.where(distance == j, COEFFS[j], weight)
    return lax.dot_general(
        delta, weight, TN, precision=lax.Precision.HIGHEST, preferred_element_type=F32
    )


def lap_at(pad_ref, zc_ref, x, cy):
    center = pad_ref[x + 4, 8 : 8 + cy, :]
    total = (3.0 * COEFFS[0]) * center + zc_ref[x]
    for j in range(1, 5):
        pair = pad_ref[x + 4 - j, 8 : 8 + cy, :] + pad_ref[x + 4 + j, 8 : 8 + cy, :]
        pair = pair + (pad_ref[x + 4, 8 - j : 8 - j + cy, :] + pad_ref[x + 4, 8 + j : 8 + j + cy, :])
        pair = pair + (pltpu.roll(center, j, 1) + pltpu.roll(center, 128 - j, 1))
        total = total + COEFFS[j] * pair
    return center, total


def spread_sources(sources, out_ref):
    for group in range(out_ref.shape[0]):
        out_ref[group] = sources[:, group * 128 : (group + 1) * 128]


def source_at(source_ref, x, low):
    piece = source_ref[x // 16]
    piece = pltpu.roll(piece, lax.rem(128 - lax.rem(x, 16) * SURF, 128), 1)
    return jnp.where(low, piece, 0.0)


def center_copy(copier, hbm, pad_ref):
    cx, cy = pad_ref.shape[0] - 8, pad_ref.shape[1] - 16
    return copier.start(hbm, pad_ref.at[4 : 4 + cx, 8 : 8 + cy, :])


def start_chunks(copier, pairs, cx):
    chunks = []
    for begin in range(0, cx, CHUNK):
        part = pl.ds(begin, CHUNK)
        chunks.append([copier.start(src.at[part], dst.at[part]) for src, dst in pairs])
    return chunks


def first_kernel(
    recv_hbm, x0_hbm, x1_hbm, y0_hbm, y1_hbm, z_hbm, z0_hbm, z1_hbm,
    now_hbm, late_hbm, courant_hbm,
    fresh_hbm, source_hbm, xs0_hbm, xs1_hbm, ys0_hbm, ys1_hbm, zs_hbm,
    recv_ref, pad_ref, y0_ref, y1_ref, z_ref, z0_ref, z1_ref, zc_ref, late_ref, courant_ref,
    fresh_ref, source_ref, later_ref, ys0_ref, ys1_ref, zs_ref, sems,
):
    cx, cy, cz = fresh_ref.shape
    copier = Copier(sems)
    recv = copier.start(recv_hbm, recv_ref)
    halo = start_halo(
        copier, pad_ref, (x0_hbm, x1_hbm, y0_hbm, y1_hbm, z_hbm, z0_hbm, z1_hbm),
        (y0_ref, y1_ref, z_ref, z0_ref, z1_ref),
    )
    now = center_copy(copier, now_hbm, pad_ref)
    chunks = start_chunks(copier, ((late_hbm, late_ref), (courant_hbm, courant_ref)), cx)
    recv.wait()
    sources, later = bin_records(recv_ref, cx, cy, cz)
    spread_sources(sources, source_ref)
    spread_sources(later, later_ref)
    copier.send(later_ref, source_hbm)
    for copy in halo:
        copy.wait()
    fill_xy(pad_ref, y0_ref, y1_ref)
    zc_ref[...] = depth_correction(z_ref[...], z0_ref[...], z1_ref[...]).reshape(cx, cy, cz)
    now.wait()
    low = iota((cy, cz), 1) < SURF

    def body(x, carry):
        center, lap = lap_at(pad_ref, zc_ref, x, cy)
        lap = lap + source_at(source_ref, x, low)
        fresh_ref[x] = 2.0 * center - late_ref[x] + courant_ref[x] * lap
        return carry

    for c, copies in enumerate(chunks):
        for copy in copies:
            copy.wait()
        part = pl.ds(c * CHUNK, CHUNK)
        lax.fori_loop(c * CHUNK, (c + 1) * CHUNK, body, 0, unroll=UNROLL)
        copier.send(fresh_ref.at[part], fresh_hbm.at[part])
    for src, dst in zip(x_faces(fresh_ref), (xs0_hbm, xs1_hbm)):
        copier.send(src, dst)
    store_y_faces(fresh_ref, ys0_ref, ys1_ref)
    copier.send(ys0_ref, ys0_hbm)
    copier.send(ys1_ref, ys1_hbm)
    zs_ref[...] = depth_faces(fresh_ref[...].reshape(cx * cy, cz))
    copier.send(zs_ref, zs_hbm)
    copier.close()


def second_kernel(
    now_hbm, source_hbm, x0_hbm, x1_hbm, y0_hbm, y1_hbm, z_hbm, z0_hbm, z1_hbm,
    late_hbm, courant_hbm, forward_hbm, image_hbm,
    fresh_hbm, image_out_hbm,
    source_ref, pad_ref, y0_ref, y1_ref, z_ref, z0_ref, z1_ref, zc_ref, late_ref, courant_ref,
    forward0_ref, forward1_ref, image_ref, fresh_ref, sems,
):
    cx, cy, cz = fresh_ref.shape
    copier = Copier(sems)
    halo = start_halo(
        copier, pad_ref, (x0_hbm, x1_hbm, y0_hbm, y1_hbm, z_hbm, z0_hbm, z1_hbm),
        (y0_ref, y1_ref, z_ref, z0_ref, z1_ref),
    )
    now = center_copy(copier, now_hbm, pad_ref)
    source = copier.start(source_hbm, source_ref)
    chunks = start_chunks(
        copier,
        (
            (late_hbm, late_ref), (courant_hbm, courant_ref), (image_hbm, image_ref),
            (forward_hbm.at[0], forward0_ref), (forward_hbm.at[1], forward1_ref),
        ),
        cx,
    )
    for copy in halo:
        copy.wait()
    fill_xy(pad_ref, y0_ref, y1_ref)
    zc_ref[...] = depth_correction(z_ref[...], z0_ref[...], z1_ref[...]).reshape(cx, cy, cz)
    now.wait()
    source.wait()
    low = iota((cy, cz), 1) < SURF

    def body(x, carry):
        center, lap = lap_at(pad_ref, zc_ref, x, cy)
        lap = lap + source_at(source_ref, x, low)
        fresh = 2.0 * center - late_ref[x] + courant_ref[x] * lap
        fresh_ref[x] = fresh
        image = image_ref[x] + forward0_ref[x].astype(F32) * center
        image_ref[x] = image + forward1_ref[x].astype(F32) * fresh
        return carry

    for c, copies in enumerate(chunks):
        for copy in copies:
            copy.wait()
        part = pl.ds(c * CHUNK, CHUNK)
        lax.fori_loop(c * CHUNK, (c + 1) * CHUNK, body, 0, unroll=UNROLL)
        copier.send(fresh_ref.at[part], fresh_hbm.at[part])
        copier.send(image_ref.at[part], image_out_hbm.at[part])
    copier.close()


def turn(value, axis, by):
    count = lax.axis_size(axis)
    return lax.ppermute(value, axis, [(i, (i + by) % count) for i in range(count)])


def exchange(x_low, x_high, y_low, y_high, z):
    return (
        turn(x_high, "gx", 1), turn(x_low, "gx", -1),
        turn(y_high, "gy", 1), turn(y_low, "gy", -1),
        z, turn(z, "gz", 1), turn(z, "gz", -1),
    )


def struct(*shape):
    return jax.ShapeDtypeStruct(shape, F32)


def vm(*shape, dtype=F32):
    return pltpu.VMEM(shape, dtype)


def call(kernel, outs, args, scratch, copies):
    anywhere = pl.BlockSpec(memory_space=pl.ANY)
    size = sum(a.size * a.dtype.itemsize for a in args) + sum(o.size * 4 for o in outs)
    return pl.pallas_call(
        kernel,
        out_shape=outs,
        in_specs=[anywhere] * len(args),
        out_specs=[anywhere] * len(outs),
        scratch_shapes=list(scratch) + [pltpu.SemaphoreType.DMA((copies,))],
        compiler_params=pltpu.CompilerParams(vmem_limit_bytes=60 * 2**20),
        cost_estimate=pl.CostEstimate(flops=10**10, bytes_accessed=size, transcendentals=0),
    )(*args)


def on_device(adjoint_now, adjoint_late, courant, forward, image_in, traces, rec_owner, rec_cell):
    cx, cy, cz = adjoint_now.shape
    n_gy, n_gz = lax.axis_size("gy"), lax.axis_size("gz")
    chunks = rec_owner.shape[0] // 128
    groups = -(-cx * SURF // 128)
    block = struct(cx, cy, cz)
    x_face, y_face = struct(4, cy, cz), struct(cx // 2, 8, cz)
    faces = (x_face, x_face, y_face, y_face, struct(8, cx * cy))
    grid, y_in, z_in = vm(cx, cy, cz), vm(cx // 2, 8, cz), vm(8, cx * cy)
    pad = vm(cx + 8, cy + 16, cz)
    slots = (n_gy * n_gz, 2, 128)
    packed, *out_faces = call(
        functools.partial(send_kernel, n_gy, n_gz), (struct(*slots),) + faces,
        (traces, rec_owner.reshape(chunks, 128), rec_cell.reshape(chunks, 128), adjoint_now),
        (
            vm(*traces.shape), vm(chunks, 128, dtype=jnp.int32), vm(chunks, 128, dtype=jnp.int32),
            grid, vm(*slots), y_in, y_in, z_in,
        ),
        10,
    )
    received = lax.all_to_all(packed, ("gz", "gy"), 0, 0)
    halo = exchange(*out_faces)
    turns = cx // CHUNK
    source = (groups, cy, 128)
    middle, later, *out_faces = call(
        first_kernel, (block, struct(*source)) + faces,
        (received,) + halo + (adjoint_now, adjoint_late, courant),
        (
            vm(*slots), pad, y_in, y_in, z_in, z_in, z_in, grid, grid, grid,
            grid, vm(*source), vm(*source), y_in, y_in, z_in,
        ),
        15 + 3 * turns,
    )
    halo = exchange(*out_faces)
    half = vm(cx, cy, cz, dtype=BF16)
    newest, image = call(
        second_kernel, (block, block),
        (middle, later) + halo + (adjoint_now, courant, forward, image_in),
        (
            vm(*source), pad, y_in, y_in, z_in, z_in, z_in, grid, grid, grid,
            half, half, grid, grid,
        ),
        9 + 7 * turns,
    )
    return newest, middle, image


def solution(mesh):
    grid = P("gx", "gy", "gz")
    return jax.shard_map(
        on_device,
        mesh=mesh,
        in_specs=(
            grid, grid, grid, P(None, "gx", "gy", "gz"), grid,
            P(None, ("gy", "gz")), P(("gy", "gz")), P(("gy", "gz")),
        ),
        out_specs=(grid, grid, grid),
        check_vma=False,
    )
```

```python
import functools

import jax
import jax.numpy as jnp
from jax import lax
from jax.experimental import pallas as pl
from jax.experimental.pallas import tpu as pltpu
from jax.sharding import PartitionSpec as P

COEFFS = (-205.0 / 72.0, 8.0 / 5.0, -1.0 / 5.0, 8.0 / 315.0, -1.0 / 560.0)
SURF = 8
CAP = 64
CHUNK = 20
UNROLL = 20
F32 = jnp.float32
BF16 = jnp.bfloat16
NT = (((1,), (1,)), ((), ()))
TN = (((0,), (0,)), ((), ()))


def split3(value):
    high = value.astype(BF16).astype(F32)
    rest = value - high
    middle = rest.astype(BF16).astype(F32)
    return high, middle, rest - middle


def iota(shape, dim):
    return lax.broadcasted_iota(jnp.int32, shape, dim)


def pack_records(n_gy, n_gz, traces_ref, owner_ref, cell_ref, out_ref):
    me = lax.axis_index("gx")
    chunks = owner_ref.shape[0]
    owner_ids = iota((n_gy, 128), 0)
    picks = []
    for c in range(chunks):
        owner = owner_ref[c : c + 1, :]
        local = owner - me * (n_gy * n_gz)
        dest = lax.shift_right_arithmetic(local, n_gz.bit_length() - 1)
        picks.append(jnp.where(owner_ids == dest, 1.0, 0.0).astype(F32))
    all_picks = jnp.concatenate(picks, axis=0)
    before = (iota((128, 128), 0) < iota((128, 128), 1)).astype(F32).astype(BF16)
    prefix = jnp.dot(all_picks.astype(BF16), before, preferred_element_type=F32)
    offset = jnp.zeros((n_gy, 1), F32)
    slot_ids = iota((128, 128), 0)
    slots_low, slots_high, left, right = [], [], [], []
    for c in range(chunks):
        pick = picks[c]
        rank = jnp.sum(pick * (prefix[c * n_gy : (c + 1) * n_gy] + offset), axis=0, keepdims=True)
        offset = offset + jnp.sum(pick, axis=1, keepdims=True)
        rank = rank.astype(jnp.int32)
        slots_low.append(jnp.where(slot_ids == rank, 1.0, 0.0).astype(BF16))
        slots_high.append(jnp.where(slot_ids == rank + CAP, 1.0, 0.0).astype(BF16))
        first = traces_ref[0:1, c * 128 : (c + 1) * 128]
        second = traces_ref[1:2, c * 128 : (c + 1) * 128]
        cell = cell_ref[c : c + 1, :].astype(F32)
        left.append(
            jnp.concatenate([pick * s for s in split3(first) + split3(cell)], axis=0).astype(BF16)
        )
        right.append(jnp.concatenate([pick * s for s in split3(second)], axis=0).astype(BF16))
    low = jnp.concatenate(slots_low, axis=1)
    high = jnp.concatenate(slots_high, axis=1)
    left = lax.dot_general(jnp.concatenate(left, axis=1), low, NT, preferred_element_type=F32)
    right = lax.dot_general(jnp.concatenate(right, axis=1), high, NT, preferred_element_type=F32)

    def joined(value, at):
        parts = [value[(at + i) * n_gy : (at + i + 1) * n_gy] for i in range(3)]
        return parts[0] + parts[1] + parts[2]

    values = joined(left, 0) + joined(right, 0)
    cells = joined(left, 3)
    out_ref[...] = jnp.zeros_like(out_ref)
    for d in range(n_gy):
        out_ref[d, 0:1, :] = values[d : d + 1, :]
        out_ref[d, 1:2, :] = cells[d : d + 1, :]


def store_y_faces(src_ref, low_ref, high_ref):
    cx, cy, _ = src_ref.shape
    half = cx // 2
    for x in range(half):
        one, two = src_ref[x], src_ref[x + half]
        low_ref[x] = jnp.concatenate([one[0:4], two[0:4]], axis=0)
        high_ref[x] = jnp.concatenate([one[cy - 4 : cy], two[cy - 4 : cy]], axis=0)


def x_faces(ref):
    cx = ref.shape[0]
    return ref.at[0:4], ref.at[cx - 4 : cx]


def at_edges(axis):
    at = lax.axis_index(axis)
    return at == 0, at == lax.axis_size(axis) - 1


class Copier:
    def __init__(self, sems):
        self.sems, self.used, self.open = sems, 0, []

    def start(self, src, dst):
        copy = pltpu.make_async_copy(src, dst, self.sems.at[self.used])
        self.used += 1
        copy.start()
        return copy

    def send(self, src, dst):
        self.open.append(self.start(src, dst))

    def close(self):
        for copy in self.open:
            copy.wait()


def depth_faces(value):
    at = iota((8, 128), 0)
    take = iota((8, 128), 1) == jnp.where(at < 4, at, at + 120)
    take = jnp.where(take, 1.0, 0.0).astype(BF16)
    parts = [
        lax.dot_general(take, s.astype(BF16), NT, preferred_element_type=F32) for s in split3(value)
    ]
    return parts[0] + parts[1] + parts[2]


def send_kernel(
    n_gy, n_gz, traces_hbm, owner_hbm, cell_hbm, now_hbm,
    packed_hbm, x0_hbm, x1_hbm, y0_hbm, y1_hbm, z_hbm,
    traces_ref, owner_ref, cell_ref, now_ref, packed_ref, y0_ref, y1_ref, z_ref, sems,
):
    cx, cy, cz = now_ref.shape
    copier = Copier(sems)
    pairs = ((traces_hbm, traces_ref), (owner_hbm, owner_ref), (cell_hbm, cell_ref))
    records = [copier.start(src, dst) for src, dst in pairs]
    now = copier.start(now_hbm, now_ref)
    for copy in records:
        copy.wait()
    pack_records(n_gy, n_gz, traces_ref, owner_ref, cell_ref, packed_ref)
    copier.send(packed_ref, packed_hbm)
    now.wait()
    for src, dst in zip(x_faces(now_ref), (x0_hbm, x1_hbm)):
        copier.send(src, dst)
    store_y_faces(now_ref, y0_ref, y1_ref)
    copier.send(y0_ref, y0_hbm)
    copier.send(y1_ref, y1_hbm)
    z_ref[...] = depth_faces(now_ref[...].reshape(cx * cy, cz))
    copier.send(z_ref, z_hbm)
    copier.close()


def bin_records(recv_ref, cx, cy, cz):
    senders = recv_ref.shape[0]
    half = senders // 2
    values = recv_ref[:, 0, :]
    cells = recv_ref[:, 1, :]
    low = iota((half, 128), 1) < CAP
    rolled = pltpu.roll(values, CAP, 1)
    first = jnp.where(low, values[:half], rolled[half:])
    second = jnp.where(low, rolled[:half], values[half:])
    cell = jnp.where(low, cells[:half], pltpu.roll(cells, CAP, 1)[half:]).astype(jnp.int32)
    depth = lax.bitwise_and(cell, cz - 1)
    plane = lax.shift_right_logical(cell, cz.bit_length() - 1)
    at_x = plane // cy
    at_y = plane - at_x * cy
    column = at_x * SURF + depth
    columns = -(-cx * SURF // 128) * 128
    pieces = split3(first) + split3(second)
    row_ids = iota((cy, 128), 0)
    column_ids = iota((columns, 128), 0)
    total = None
    step = 4
    for begin in range(0, half, step):
        lefts, rights = [], []
        for s in range(begin, begin + step):
            hit = row_ids == at_y[s : s + 1]
            lefts.append(
                jnp.concatenate([jnp.where(hit, p[s : s + 1], 0.0) for p in pieces], axis=0).astype(BF16)
            )
            rights.append(jnp.where(column_ids == column[s : s + 1], 1.0, 0.0).astype(BF16))
        term = lax.dot_general(
            jnp.concatenate(lefts, axis=1), jnp.concatenate(rights, axis=1), NT,
            preferred_element_type=F32,
        )
        total = term if total is None else total + term
    part = [total[i * cy : (i + 1) * cy] for i in range(6)]
    return part[0] + part[1] + part[2], part[3] + part[4] + part[5]


def start_halo(copier, pad_ref, halo_hbm, halo_refs):
    cx, cy = pad_ref.shape[0] - 8, pad_ref.shape[1] - 16
    places = (pad_ref.at[0:4, 8 : 8 + cy, :], pad_ref.at[4 + cx : 8 + cx, 8 : 8 + cy, :])
    return [copier.start(src, dst) for src, dst in zip(halo_hbm, places + tuple(halo_refs))]


def fill_xy(pad_ref, before_ref, after_ref):
    cx, cy, cz = pad_ref.shape[0] - 8, pad_ref.shape[1] - 16, pad_ref.shape[2]
    half = cx // 2
    for edge, begin in zip(at_edges("gx"), (0, 4 + cx)):

        @pl.when(edge)
        def _(begin=begin):
            pad_ref[begin : begin + 4, 8 : 8 + cy, :] = jnp.zeros((4, cy, cz), F32)

    first, last = at_edges("gy")
    for x in range(half):
        before = jnp.where(first, 0.0, before_ref[x])
        after = jnp.where(last, 0.0, after_ref[x])
        pad_ref[4 + x, 4:8, :] = before[0:4]
        pad_ref[4 + half + x, 4:8, :] = before[4:8]
        pad_ref[4 + x, 8 + cy : 12 + cy, :] = after[0:4]
        pad_ref[4 + half + x, 8 + cy : 12 + cy, :] = after[4:8]


def depth_correction(own, before, after):
    at = iota(own.shape, 0)
    first, last = at_edges("gz")
    delta = jnp.where(at < 4, jnp.where(last, 0.0, after), jnp.where(first, 0.0, before)) - own
    row = iota((8, 128), 0)
    lane = iota((8, 128), 1)
    distance = jnp.where(row < 4, 128 + row - lane, lane + 8 - row)
    weight = jnp.zeros((8, 128), F32)
    for j in range(1, 5):
        weight = jnp.where(distance == j, COEFFS[j], weight)
    d, w = split3(delta), split3(weight)
    left = jnp.concatenate([d[0], d[1], d[2], d[0], d[1], d[0]], axis=0).astype(BF16)
    right = jnp.concatenate([w[0], w[0], w[0], w[1], w[1], w[2]], axis=0).astype(BF16)
    return lax.dot_general(left, right, TN, preferred_element_type=F32)


def lap_at(pad_ref, zc_ref, x, cy):
    center = pad_ref[x + 4, 8 : 8 + cy, :]
    total = (3.0 * COEFFS[0]) * center + zc_ref[x]
    for j in range(1, 5):
        pair = pad_ref[x + 4 - j, 8 : 8 + cy, :] + pad_ref[x + 4 + j, 8 : 8 + cy, :]
        pair = pair + (pad_ref[x + 4, 8 - j : 8 - j + cy, :] + pad_ref[x + 4, 8 + j : 8 + j + cy, :])
        pair = pair + (pltpu.roll(center, j, 1) + pltpu.roll(center, 128 - j, 1))
        total = total + COEFFS[j] * pair
    return center, total


def spread_sources(sources, out_ref):
    for group in range(out_ref.shape[0]):
        out_ref[group] = sources[:, group * 128 : (group + 1) * 128]


def source_at(source_ref, x, low):
    piece = source_ref[x // 16]
    piece = pltpu.roll(piece, lax.rem(128 - lax.rem(x, 16) * SURF, 128), 1)
    return jnp.where(low, piece, 0.0)


def center_copy(copier, hbm, pad_ref):
    cx, cy = pad_ref.shape[0] - 8, pad_ref.shape[1] - 16
    return copier.start(hbm, pad_ref.at[4 : 4 + cx, 8 : 8 + cy, :])


def start_chunks(copier, pairs, cx):
    chunks = []
    for begin in range(0, cx, CHUNK):
        part = pl.ds(begin, CHUNK)
        chunks.append([copier.start(src.at[part], dst.at[part]) for src, dst in pairs])
    return chunks


def first_kernel(
    recv_hbm, x0_hbm, x1_hbm, y0_hbm, y1_hbm, z_hbm, z0_hbm, z1_hbm,
    now_hbm, late_hbm, courant_hbm,
    fresh_hbm, source_hbm, xs0_hbm, xs1_hbm, ys0_hbm, ys1_hbm, zs_hbm,
    recv_ref, pad_ref, y0_ref, y1_ref, z_ref, z0_ref, z1_ref, zc_ref, late_ref, courant_ref,
    fresh_ref, source_ref, later_ref, ys0_ref, ys1_ref, zs_ref, sems,
):
    cx, cy, cz = fresh_ref.shape
    copier = Copier(sems)
    recv = copier.start(recv_hbm, recv_ref)
    halo = start_halo(
        copier, pad_ref, (x0_hbm, x1_hbm, y0_hbm, y1_hbm, z_hbm, z0_hbm, z1_hbm),
        (y0_ref, y1_ref, z_ref, z0_ref, z1_ref),
    )
    now = center_copy(copier, now_hbm, pad_ref)
    chunks = start_chunks(copier, ((late_hbm, late_ref), (courant_hbm, courant_ref)), cx)
    recv.wait()
    sources, later = bin_records(recv_ref, cx, cy, cz)
    spread_sources(sources, source_ref)
    spread_sources(later, later_ref)
    copier.send(later_ref, source_hbm)
    for copy in halo:
        copy.wait()
    fill_xy(pad_ref, y0_ref, y1_ref)
    zc_ref[...] = depth_correction(z_ref[...], z0_ref[...], z1_ref[...]).reshape(cx, cy, cz)
    now.wait()
    low = iota((cy, cz), 1) < SURF

    def body(x, carry):
        center, lap = lap_at(pad_ref, zc_ref, x, cy)
        lap = lap + source_at(source_ref, x, low)
        fresh_ref[x] = 2.0 * center - late_ref[x] + courant_ref[x] * lap
        return carry

    for c, copies in enumerate(chunks):
        for copy in copies:
            copy.wait()
        part = pl.ds(c * CHUNK, CHUNK)
        lax.fori_loop(c * CHUNK, (c + 1) * CHUNK, body, 0, unroll=UNROLL)
        copier.send(fresh_ref.at[part], fresh_hbm.at[part])
    for src, dst in zip(x_faces(fresh_ref), (xs0_hbm, xs1_hbm)):
        copier.send(src, dst)
    store_y_faces(fresh_ref, ys0_ref, ys1_ref)
    copier.send(ys0_ref, ys0_hbm)
    copier.send(ys1_ref, ys1_hbm)
    zs_ref[...] = depth_faces(fresh_ref[...].reshape(cx * cy, cz))
    copier.send(zs_ref, zs_hbm)
    copier.close()


def second_kernel(
    now_hbm, source_hbm, x0_hbm, x1_hbm, y0_hbm, y1_hbm, z_hbm, z0_hbm, z1_hbm,
    late_hbm, courant_hbm, forward_hbm, image_hbm,
    fresh_hbm, image_out_hbm,
    source_ref, pad_ref, y0_ref, y1_ref, z_ref, z0_ref, z1_ref, zc_ref, late_ref, courant_ref,
    forward0_ref, forward1_ref, image_ref, fresh_ref, sems,
):
    cx, cy, cz = fresh_ref.shape
    copier = Copier(sems)
    halo = start_halo(
        copier, pad_ref, (x0_hbm, x1_hbm, y0_hbm, y1_hbm, z_hbm, z0_hbm, z1_hbm),
        (y0_ref, y1_ref, z_ref, z0_ref, z1_ref),
    )
    now = center_copy(copier, now_hbm, pad_ref)
    source = copier.start(source_hbm, source_ref)
    chunks = start_chunks(
        copier,
        (
            (late_hbm, late_ref), (courant_hbm, courant_ref), (image_hbm, image_ref),
            (forward_hbm.at[0], forward0_ref), (forward_hbm.at[1], forward1_ref),
        ),
        cx,
    )
    for copy in halo:
        copy.wait()
    fill_xy(pad_ref, y0_ref, y1_ref)
    zc_ref[...] = depth_correction(z_ref[...], z0_ref[...], z1_ref[...]).reshape(cx, cy, cz)
    now.wait()
    source.wait()
    low = iota((cy, cz), 1) < SURF

    def body(x, carry):
        center, lap = lap_at(pad_ref, zc_ref, x, cy)
        lap = lap + source_at(source_ref, x, low)
        fresh = 2.0 * center - late_ref[x] + courant_ref[x] * lap
        fresh_ref[x] = fresh
        image = image_ref[x] + forward0_ref[x].astype(F32) * center
        image_ref[x] = image + forward1_ref[x].astype(F32) * fresh
        return carry

    for c, copies in enumerate(chunks):
        for copy in copies:
            copy.wait()
        part = pl.ds(c * CHUNK, CHUNK)
        lax.fori_loop(c * CHUNK, (c + 1) * CHUNK, body, 0, unroll=UNROLL)
        copier.send(fresh_ref.at[part], fresh_hbm.at[part])
        copier.send(image_ref.at[part], image_out_hbm.at[part])
    copier.close()


def turn(value, axis, by):
    count = lax.axis_size(axis)
    return lax.ppermute(value, axis, [(i, (i + by) % count) for i in range(count)])


def exchange(x_low, x_high, y_low, y_high, z):
    z_before, z_after = turn(z, "gz", 1), turn(z, "gz", -1)
    y_before, y_after = turn(y_high, "gy", 1), turn(y_low, "gy", -1)
    x_before = turn(x_high, "gx", 1)
    x_low, z_before, z_after = lax.optimization_barrier((x_low, z_before, z_after))
    x_after = turn(x_low, "gx", -1)
    return x_before, x_after, y_before, y_after, z, z_before, z_after


def struct(*shape):
    return jax.ShapeDtypeStruct(shape, F32)


def vm(*shape, dtype=F32):
    return pltpu.VMEM(shape, dtype)


def call(kernel, outs, args, scratch, copies):
    anywhere = pl.BlockSpec(memory_space=pl.ANY)
    size = sum(a.size * a.dtype.itemsize for a in args) + sum(o.size * 4 for o in outs)
    return pl.pallas_call(
        kernel,
        out_shape=outs,
        in_specs=[anywhere] * len(args),
        out_specs=[anywhere] * len(outs),
        scratch_shapes=list(scratch) + [pltpu.SemaphoreType.DMA((copies,))],
        compiler_params=pltpu.CompilerParams(vmem_limit_bytes=63_480_000),
        cost_estimate=pl.CostEstimate(flops=10**10, bytes_accessed=size, transcendentals=0),
    )(*args)


def on_device(adjoint_now, adjoint_late, courant, forward, image_in, traces, rec_owner, rec_cell):
    cx, cy, cz = adjoint_now.shape
    n_gy, n_gz = lax.axis_size("gy"), lax.axis_size("gz")
    chunks = rec_owner.shape[0] // 128
    groups = -(-cx * SURF // 128)
    block = struct(cx, cy, cz)
    x_face, y_face = struct(4, cy, cz), struct(cx // 2, 8, cz)
    faces = (x_face, x_face, y_face, y_face, struct(8, cx * cy))
    grid, y_in, z_in = vm(cx, cy, cz), vm(cx // 2, 8, cz), vm(8, cx * cy)
    pad = vm(cx + 8, cy + 16, cz)
    slots = (n_gy * n_gz, 2, 128)
    packed, *out_faces = call(
        functools.partial(send_kernel, n_gy, n_gz), (struct(*slots),) + faces,
        (traces, rec_owner.reshape(chunks, 128), rec_cell.reshape(chunks, 128), adjoint_now),
        (
            vm(*traces.shape), vm(chunks, 128, dtype=jnp.int32), vm(chunks, 128, dtype=jnp.int32),
            grid, vm(*slots), y_in, y_in, z_in,
        ),
        10,
    )
    received = lax.all_to_all(packed, ("gz", "gy"), 0, 0)
    halo = exchange(*out_faces)
    turns = cx // CHUNK
    source = (groups, cy, 128)
    middle, later, *out_faces = call(
        first_kernel, (block, struct(*source)) + faces,
        (received,) + halo + (adjoint_now, adjoint_late, courant),
        (
            vm(*slots), pad, y_in, y_in, z_in, z_in, z_in, grid, grid, grid,
            grid, vm(*source), vm(*source), y_in, y_in, z_in,
        ),
        15 + 3 * turns,
    )
    halo = exchange(*out_faces)
    half = vm(cx, cy, cz, dtype=BF16)
    newest, image = call(
        second_kernel, (block, block),
        (middle, later) + halo + (adjoint_now, courant, forward, image_in),
        (
            vm(*source), pad, y_in, y_in, z_in, z_in, z_in, grid, grid, grid,
            half, half, grid, grid,
        ),
        9 + 7 * turns,
    )
    return newest, middle, image


def solution(mesh):
    grid = P("gx", "gy", "gz")
    return jax.shard_map(
        on_device,
        mesh=mesh,
        in_specs=(
            grid, grid, grid, P(None, "gx", "gy", "gz"), grid,
            P(None, ("gy", "gz")), P(("gy", "gz")), P(("gy", "gz")),
        ),
        out_specs=(grid, grid, grid),
        check_vma=False,
    )
```

```python
import functools

import jax
import jax.numpy as jnp
from jax import lax
from jax.experimental import pallas as pl
from jax.experimental.pallas import tpu as pltpu
from jax.sharding import PartitionSpec as P

COEFFS = (-205.0 / 72.0, 8.0 / 5.0, -1.0 / 5.0, 8.0 / 315.0, -1.0 / 560.0)
SURF = 8
CAP = 64
CHUNK = 20
F32 = jnp.float32
BF16 = jnp.bfloat16
NT = (((1,), (1,)), ((), ()))
TN = (((0,), (0,)), ((), ()))


def split3(value):
    high = value.astype(BF16).astype(F32)
    rest = value - high
    middle = rest.astype(BF16).astype(F32)
    return high, middle, rest - middle


def iota(shape, dim):
    return lax.broadcasted_iota(jnp.int32, shape, dim)


def pack_records(n_gy, n_gz, traces_ref, owner_ref, cell_ref, out_ref):
    me = lax.axis_index("gx")
    chunks = owner_ref.shape[0]
    owner_ids = iota((n_gy, 128), 0)
    picks = []
    for c in range(chunks):
        owner = owner_ref[c : c + 1, :]
        local = owner - me * (n_gy * n_gz)
        dest = lax.shift_right_arithmetic(local, n_gz.bit_length() - 1)
        picks.append(jnp.where(owner_ids == dest, 1.0, 0.0).astype(F32))
    all_picks = jnp.concatenate(picks, axis=0)
    before = (iota((128, 128), 0) < iota((128, 128), 1)).astype(F32).astype(BF16)
    prefix = jnp.dot(all_picks.astype(BF16), before, preferred_element_type=F32)
    offset = jnp.zeros((n_gy, 1), F32)
    slot_ids = iota((128, 128), 0)
    slots_low, slots_high, left, right = [], [], [], []
    for c in range(chunks):
        pick = picks[c]
        rank = jnp.sum(pick * (prefix[c * n_gy : (c + 1) * n_gy] + offset), axis=0, keepdims=True)
        offset = offset + jnp.sum(pick, axis=1, keepdims=True)
        rank = rank.astype(jnp.int32)
        slots_low.append(jnp.where(slot_ids == rank, 1.0, 0.0).astype(BF16))
        slots_high.append(jnp.where(slot_ids == rank + CAP, 1.0, 0.0).astype(BF16))
        first = traces_ref[0:1, c * 128 : (c + 1) * 128]
        second = traces_ref[1:2, c * 128 : (c + 1) * 128]
        cell = cell_ref[c : c + 1, :].astype(F32)
        left.append(
            jnp.concatenate([pick * s for s in split3(first) + split3(cell)], axis=0).astype(BF16)
        )
        right.append(jnp.concatenate([pick * s for s in split3(second)], axis=0).astype(BF16))
    low = jnp.concatenate(slots_low, axis=1)
    high = jnp.concatenate(slots_high, axis=1)
    left = lax.dot_general(jnp.concatenate(left, axis=1), low, NT, preferred_element_type=F32)
    right = lax.dot_general(jnp.concatenate(right, axis=1), high, NT, preferred_element_type=F32)

    def joined(value, at):
        parts = [value[(at + i) * n_gy : (at + i + 1) * n_gy] for i in range(3)]
        return parts[0] + parts[1] + parts[2]

    values = joined(left, 0) + joined(right, 0)
    cells = joined(left, 3)
    out_ref[...] = jnp.zeros_like(out_ref)
    for d in range(n_gy):
        out_ref[d, 0:1, :] = values[d : d + 1, :]
        out_ref[d, 1:2, :] = cells[d : d + 1, :]


def store_y_faces(src_ref, low_ref, high_ref):
    cx, cy, _ = src_ref.shape
    half = cx // 2
    for x in range(half):
        one, two = src_ref[x], src_ref[x + half]
        low_ref[x] = jnp.concatenate([one[0:4], two[0:4]], axis=0)
        high_ref[x] = jnp.concatenate([one[cy - 4 : cy], two[cy - 4 : cy]], axis=0)


def x_faces(ref):
    cx = ref.shape[0]
    return ref.at[0:4], ref.at[cx - 4 : cx]


def at_edges(axis):
    at = lax.axis_index(axis)
    return at == 0, at == lax.axis_size(axis) - 1


class Copier:
    def __init__(self, sems):
        self.sems, self.used, self.open = sems, 0, []

    def start(self, src, dst):
        copy = pltpu.make_async_copy(src, dst, self.sems.at[self.used])
        self.used += 1
        copy.start()
        return copy

    def send(self, src, dst):
        self.open.append(self.start(src, dst))

    def close(self):
        for copy in self.open:
            copy.wait()


def depth_rows(cx, cy):
    return -(-cx * cy // 128) * 8


def depth_faces(src_ref, out_ref):
    cx, cy, _ = src_ref.shape
    per = cy // 8
    group = lax.shift_right_logical(iota((8, 128), 1), 3)
    for begin in range(0, cx * per, 16):
        packed = jnp.zeros((8, 128), F32)
        for i in range(begin, min(begin + 16, cx * per)):
            k = i - begin
            row = src_ref[i // per, i % per * 8 : i % per * 8 + 8, :]
            packed = jnp.where(group == k, pltpu.roll(row, 4 + 8 * k, 1), packed)
        out_ref[begin // 2 : begin // 2 + 8, :] = packed


def send_kernel(
    n_gy, n_gz, traces_hbm, owner_hbm, cell_hbm, now_hbm,
    packed_hbm, x0_hbm, x1_hbm, y0_hbm, y1_hbm, z_hbm,
    traces_ref, owner_ref, cell_ref, now_ref, packed_ref, y0_ref, y1_ref, z_ref, sems,
):
    cx, cy, cz = now_ref.shape
    copier = Copier(sems)
    pairs = ((traces_hbm, traces_ref), (owner_hbm, owner_ref), (cell_hbm, cell_ref))
    records = [copier.start(src, dst) for src, dst in pairs]
    now = copier.start(now_hbm, now_ref)
    for copy in records:
        copy.wait()
    pack_records(n_gy, n_gz, traces_ref, owner_ref, cell_ref, packed_ref)
    copier.send(packed_ref, packed_hbm)
    now.wait()
    for src, dst in zip(x_faces(now_ref), (x0_hbm, x1_hbm)):
        copier.send(src, dst)
    store_y_faces(now_ref, y0_ref, y1_ref)
    copier.send(y0_ref, y0_hbm)
    copier.send(y1_ref, y1_hbm)
    depth_faces(now_ref, z_ref)
    copier.send(z_ref, z_hbm)
    copier.close()


def bin_records(recv_ref, cx, cy, cz):
    senders = recv_ref.shape[0]
    half = senders // 2
    values = recv_ref[:, 0, :]
    cells = recv_ref[:, 1, :]
    low = iota((half, 128), 1) < CAP
    rolled = pltpu.roll(values, CAP, 1)
    first = jnp.where(low, values[:half], rolled[half:])
    second = jnp.where(low, rolled[:half], values[half:])
    cell = jnp.where(low, cells[:half], pltpu.roll(cells, CAP, 1)[half:]).astype(jnp.int32)
    depth = lax.bitwise_and(cell, cz - 1)
    plane = lax.shift_right_logical(cell, cz.bit_length() - 1)
    at_x = plane // cy
    at_y = plane - at_x * cy
    column = at_x * SURF + depth
    columns = -(-cx * SURF // 128) * 128
    pieces = split3(first) + split3(second)
    row_ids = iota((cy, 128), 0)
    column_ids = iota((columns, 128), 0)
    total = None
    step = 4
    for begin in range(0, half, step):
        lefts, rights = [], []
        for s in range(begin, begin + step):
            hit = row_ids == at_y[s : s + 1]
            lefts.append(
                jnp.concatenate([jnp.where(hit, p[s : s + 1], 0.0) for p in pieces], axis=0).astype(BF16)
            )
            rights.append(jnp.where(column_ids == column[s : s + 1], 1.0, 0.0).astype(BF16))
        term = lax.dot_general(
            jnp.concatenate(lefts, axis=1), jnp.concatenate(rights, axis=1), NT,
            preferred_element_type=F32,
        )
        total = term if total is None else total + term
    part = [total[i * cy : (i + 1) * cy] for i in range(6)]
    return part[0] + part[1] + part[2], part[3] + part[4] + part[5]


def start_halo(copier, pad_ref, halo_hbm, halo_refs):
    cx, cy = pad_ref.shape[0] - 8, pad_ref.shape[1] - 16
    places = (pad_ref.at[0:4, 8 : 8 + cy, :], pad_ref.at[4 + cx : 8 + cx, 8 : 8 + cy, :])
    return [copier.start(src, dst) for src, dst in zip(halo_hbm, places + tuple(halo_refs))]


def fill_xy(pad_ref, before_ref, after_ref):
    cx, cy, cz = pad_ref.shape[0] - 8, pad_ref.shape[1] - 16, pad_ref.shape[2]
    half = cx // 2
    for edge, begin in zip(at_edges("gx"), (0, 4 + cx)):

        @pl.when(edge)
        def _(begin=begin):
            pad_ref[begin : begin + 4, 8 : 8 + cy, :] = jnp.zeros((4, cy, cz), F32)

    first, last = at_edges("gy")
    for x in range(half):
        before = jnp.where(first, 0.0, before_ref[x])
        after = jnp.where(last, 0.0, after_ref[x])
        pad_ref[4 + x, 4:8, :] = before[0:4]
        pad_ref[4 + half + x, 4:8, :] = before[4:8]
        pad_ref[4 + x, 8 + cy : 12 + cy, :] = after[0:4]
        pad_ref[4 + half + x, 8 + cy : 12 + cy, :] = after[4:8]


def depth_correction(own_ref, before_ref, after_ref, out_ref):
    own = own_ref[...]
    cell = lax.bitwise_and(iota(own.shape, 1), 7)
    first, last = at_edges("gz")
    before, after = jnp.where(first, 0.0, before_ref[...]), jnp.where(last, 0.0, after_ref[...])
    high, middle, low = split3(jnp.where(cell < 4, before, after) - own)
    source, target = iota((128, 128), 0), iota((128, 128), 1)
    near = lax.shift_right_logical(source, 3) == lax.shift_right_logical(target, 3)
    near = near & (lax.bitwise_and(source, 4) != lax.bitwise_and(target, 4))
    distance = jnp.where(near, jnp.abs(source - target), 0)
    weight = jnp.zeros((128, 128), F32)
    for j in range(1, 5):
        weight = jnp.where(distance == j, COEFFS[j], weight)
    w = split3(weight)
    left = jnp.concatenate([high, middle, low, high, middle, high], axis=1).astype(BF16)
    right = jnp.concatenate([w[0], w[0], w[0], w[1], w[1], w[2]], axis=0).astype(BF16)
    result = jnp.dot(left, right, preferred_element_type=F32)
    lane = iota((8, 128), 1)
    outer = (lane < 4) | (lane >= 124)
    for i in range(out_ref.shape[0]):
        row = result[i // 16 * 8 : i // 16 * 8 + 8]
        out_ref[i] = jnp.where(outer, pltpu.roll(row, 124 - i % 16 * 8, 1), 0.0)


def depth_weights():
    apart = jnp.abs(iota((128, 128), 0) - iota((128, 128), 1))
    apart = jnp.minimum(apart, 128 - apart)
    weight = jnp.zeros((128, 128), F32)
    for j in range(1, 5):
        weight = jnp.where(apart == j, COEFFS[j], weight)
    high, middle, _ = split3(weight)
    return jnp.concatenate([high, high, middle], axis=0).astype(BF16)


def depth_part(pad_ref, weights, begin, cy, zc_ref):
    rows = CHUNK * cy
    value = pad_ref[4 + begin : 4 + begin + CHUNK, 8 : 8 + cy, :].reshape(rows, 128)
    high, middle, _ = split3(value)
    left = jnp.concatenate([high, middle, high], axis=1).astype(BF16)
    result = jnp.dot(left, weights, preferred_element_type=F32)
    at = begin * cy // 8
    zc_ref[at : at + rows // 8] = zc_ref[at : at + rows // 8] + result.reshape(rows // 8, 8, 128)


def lap_at(pad_ref, zc_ref, x, cy):
    center = pad_ref[x + 4, 8 : 8 + cy, :]
    per = cy // 8
    total = (3.0 * COEFFS[0]) * center + zc_ref[x * per : (x + 1) * per].reshape(cy, center.shape[1])
    for j in range(1, 5):
        pair = pad_ref[x + 4 - j, 8 : 8 + cy, :] + pad_ref[x + 4 + j, 8 : 8 + cy, :]
        pair = pair + (pad_ref[x + 4, 8 - j : 8 - j + cy, :] + pad_ref[x + 4, 8 + j : 8 + j + cy, :])
        total = total + COEFFS[j] * pair
    return center, total


def spread_sources(sources, out_ref):
    for group in range(out_ref.shape[0]):
        out_ref[group] = sources[:, group * 128 : (group + 1) * 128]


def source_at(source_ref, x, low):
    piece = source_ref[x // 16]
    if x % 16:
        piece = pltpu.roll(piece, 128 - x % 16 * SURF, 1)
    return jnp.where(low, piece, 0.0)


def center_copy(copier, hbm, pad_ref):
    cx, cy = pad_ref.shape[0] - 8, pad_ref.shape[1] - 16
    return copier.start(hbm, pad_ref.at[4 : 4 + cx, 8 : 8 + cy, :])


def start_chunks(copier, pairs, cx):
    chunks = []
    for begin in range(0, cx, CHUNK):
        part = pl.ds(begin, CHUNK)
        chunks.append([copier.start(src.at[part], dst.at[part]) for src, dst in pairs])
    return chunks


def first_kernel(
    recv_hbm, x0_hbm, x1_hbm, y0_hbm, y1_hbm, z_hbm, z0_hbm, z1_hbm,
    now_hbm, late_hbm, courant_hbm,
    fresh_hbm, source_hbm, xs0_hbm, xs1_hbm, ys0_hbm, ys1_hbm, zs_hbm,
    recv_ref, pad_ref, y0_ref, y1_ref, z_ref, z0_ref, z1_ref, zc_ref, late_ref, courant_ref,
    fresh_ref, source_ref, later_ref, ys0_ref, ys1_ref, zs_ref, sems,
):
    cx, cy, cz = fresh_ref.shape
    copier = Copier(sems)
    recv = copier.start(recv_hbm, recv_ref)
    halo = start_halo(
        copier, pad_ref, (x0_hbm, x1_hbm, y0_hbm, y1_hbm, z_hbm, z0_hbm, z1_hbm),
        (y0_ref, y1_ref, z_ref, z0_ref, z1_ref),
    )
    now = center_copy(copier, now_hbm, pad_ref)
    chunks = start_chunks(copier, ((late_hbm, late_ref), (courant_hbm, courant_ref)), cx)
    recv.wait()
    sources, later = bin_records(recv_ref, cx, cy, cz)
    spread_sources(sources, source_ref)
    spread_sources(later, later_ref)
    copier.send(later_ref, source_hbm)
    for copy in halo:
        copy.wait()
    fill_xy(pad_ref, y0_ref, y1_ref)
    depth_correction(z_ref, z0_ref, z1_ref, zc_ref)
    now.wait()
    low = iota((cy, cz), 1) < SURF
    weights = depth_weights()

    def step(x):
        center, lap = lap_at(pad_ref, zc_ref, x, cy)
        lap = lap + source_at(source_ref, x, low)
        fresh_ref[x] = 2.0 * center - late_ref[x] + courant_ref[x] * lap

    for c, copies in enumerate(chunks):
        for copy in copies:
            copy.wait()
        part = pl.ds(c * CHUNK, CHUNK)
        depth_part(pad_ref, weights, c * CHUNK, cy, zc_ref)
        for x in range(c * CHUNK, (c + 1) * CHUNK):
            step(x)
        copier.send(fresh_ref.at[part], fresh_hbm.at[part])
    for src, dst in zip(x_faces(fresh_ref), (xs0_hbm, xs1_hbm)):
        copier.send(src, dst)
    store_y_faces(fresh_ref, ys0_ref, ys1_ref)
    copier.send(ys0_ref, ys0_hbm)
    copier.send(ys1_ref, ys1_hbm)
    depth_faces(fresh_ref, zs_ref)
    copier.send(zs_ref, zs_hbm)
    copier.close()


def second_kernel(
    now_hbm, source_hbm, x0_hbm, x1_hbm, y0_hbm, y1_hbm, z_hbm, z0_hbm, z1_hbm,
    late_hbm, courant_hbm, forward_hbm, image_hbm,
    fresh_hbm, image_out_hbm,
    source_ref, pad_ref, y0_ref, y1_ref, z_ref, z0_ref, z1_ref, zc_ref, late_ref, courant_ref,
    forward0_ref, forward1_ref, image_ref, fresh_ref, sems,
):
    cx, cy, cz = fresh_ref.shape
    copier = Copier(sems)
    halo = start_halo(
        copier, pad_ref, (x0_hbm, x1_hbm, y0_hbm, y1_hbm, z_hbm, z0_hbm, z1_hbm),
        (y0_ref, y1_ref, z_ref, z0_ref, z1_ref),
    )
    now = center_copy(copier, now_hbm, pad_ref)
    source = copier.start(source_hbm, source_ref)
    chunks = start_chunks(
        copier,
        (
            (late_hbm, late_ref), (courant_hbm, courant_ref), (image_hbm, image_ref),
            (forward_hbm.at[0], forward0_ref), (forward_hbm.at[1], forward1_ref),
        ),
        cx,
    )
    for copy in halo:
        copy.wait()
    fill_xy(pad_ref, y0_ref, y1_ref)
    depth_correction(z_ref, z0_ref, z1_ref, zc_ref)
    now.wait()
    source.wait()
    low = iota((cy, cz), 1) < SURF
    weights = depth_weights()

    def step(x):
        center, lap = lap_at(pad_ref, zc_ref, x, cy)
        lap = lap + source_at(source_ref, x, low)
        fresh = 2.0 * center - late_ref[x] + courant_ref[x] * lap
        fresh_ref[x] = fresh
        image = image_ref[x] + forward0_ref[x].astype(F32) * center
        image_ref[x] = image + forward1_ref[x].astype(F32) * fresh

    for c, copies in enumerate(chunks):
        for copy in copies:
            copy.wait()
        part = pl.ds(c * CHUNK, CHUNK)
        depth_part(pad_ref, weights, c * CHUNK, cy, zc_ref)
        for x in range(c * CHUNK, (c + 1) * CHUNK):
            step(x)
        copier.send(fresh_ref.at[part], fresh_hbm.at[part])
        copier.send(image_ref.at[part], image_out_hbm.at[part])
    copier.close()


def turn(value, axis, by):
    count = lax.axis_size(axis)
    return lax.ppermute(value, axis, [(i, (i + by) % count) for i in range(count)])


def exchange(x_low, x_high, y_low, y_high, z):
    z_before, z_after = turn(z, "gz", 1), turn(z, "gz", -1)
    y_before, y_after = turn(y_high, "gy", 1), turn(y_low, "gy", -1)
    x_before = turn(x_high, "gx", 1)
    x_low, z_before, z_after = lax.optimization_barrier((x_low, z_before, z_after))
    x_after = turn(x_low, "gx", -1)
    return x_before, x_after, y_before, y_after, z, z_before, z_after


def struct(*shape):
    return jax.ShapeDtypeStruct(shape, F32)


def vm(*shape, dtype=F32):
    return pltpu.VMEM(shape, dtype)


def call(kernel, outs, args, scratch, copies):
    anywhere = pl.BlockSpec(memory_space=pl.ANY)
    size = sum(a.size * a.dtype.itemsize for a in args) + sum(o.size * 4 for o in outs)
    return pl.pallas_call(
        kernel,
        out_shape=outs,
        in_specs=[anywhere] * len(args),
        out_specs=[anywhere] * len(outs),
        scratch_shapes=list(scratch) + [pltpu.SemaphoreType.DMA((copies,))],
        compiler_params=pltpu.CompilerParams(vmem_limit_bytes=63_480_000),
        cost_estimate=pl.CostEstimate(flops=10**10, bytes_accessed=size, transcendentals=0),
    )(*args)


def on_device(adjoint_now, adjoint_late, courant, forward, image_in, traces, rec_owner, rec_cell):
    cx, cy, cz = adjoint_now.shape
    n_gy, n_gz = lax.axis_size("gy"), lax.axis_size("gz")
    chunks = rec_owner.shape[0] // 128
    groups = -(-cx * SURF // 128)
    block = struct(cx, cy, cz)
    x_face, y_face = struct(4, cy, cz), struct(cx // 2, 8, cz)
    faces = (x_face, x_face, y_face, y_face, struct(depth_rows(cx, cy), 128))
    grid, y_in, z_in = vm(cx, cy, cz), vm(cx // 2, 8, cz), vm(depth_rows(cx, cy), 128)
    pad = vm(cx + 8, cy + 16, cz)
    corrections = vm(cx * cy // 8, 8, cz)
    slots = (n_gy * n_gz, 2, 128)
    packed, *out_faces = call(
        functools.partial(send_kernel, n_gy, n_gz), (struct(*slots),) + faces,
        (traces, rec_owner.reshape(chunks, 128), rec_cell.reshape(chunks, 128), adjoint_now),
        (
            vm(*traces.shape), vm(chunks, 128, dtype=jnp.int32), vm(chunks, 128, dtype=jnp.int32),
            grid, vm(*slots), y_in, y_in, z_in,
        ),
        10,
    )
    received = lax.all_to_all(packed, ("gz", "gy"), 0, 0)
    halo = exchange(*out_faces)
    turns = cx // CHUNK
    source = (groups, cy, 128)
    middle, later, *out_faces = call(
        first_kernel, (block, struct(*source)) + faces,
        (received,) + halo + (adjoint_now, adjoint_late, courant),
        (
            vm(*slots), pad, y_in, y_in, z_in, z_in, z_in, corrections, grid, grid,
            grid, vm(*source), vm(*source), y_in, y_in, z_in,
        ),
        15 + 3 * turns,
    )
    halo = exchange(*out_faces)
    half = vm(cx, cy, cz, dtype=BF16)
    newest, image = call(
        second_kernel, (block, block),
        (middle, later) + halo + (adjoint_now, courant, forward, image_in),
        (
            vm(*source), pad, y_in, y_in, z_in, z_in, z_in, corrections, grid, grid,
            half, half, grid, grid,
        ),
        9 + 7 * turns,
    )
    return newest, middle, image


def solution(mesh):
    grid = P("gx", "gy", "gz")
    return jax.shard_map(
        on_device,
        mesh=mesh,
        in_specs=(
            grid, grid, grid, P(None, "gx", "gy", "gz"), grid,
            P(None, ("gy", "gz")), P(("gy", "gz")), P(("gy", "gz")),
        ),
        out_specs=(grid, grid, grid),
        check_vma=False,
    )
```

```python
import functools

import jax
import jax.numpy as jnp
from jax import lax
from jax.experimental import pallas as pl
from jax.experimental.pallas import tpu as pltpu
from jax.sharding import PartitionSpec as P

COEFFS = (-205.0 / 72.0, 8.0 / 5.0, -1.0 / 5.0, 8.0 / 315.0, -1.0 / 560.0)
SURF = 8
CAP = 64
CHUNK = 20
F32 = jnp.float32
BF16 = jnp.bfloat16
NT = (((1,), (1,)), ((), ()))
TN = (((0,), (0,)), ((), ()))


def split3(value):
    high = value.astype(BF16).astype(F32)
    rest = value - high
    middle = rest.astype(BF16).astype(F32)
    return high, middle, rest - middle


def iota(shape, dim):
    return lax.broadcasted_iota(jnp.int32, shape, dim)


def pack_records(n_gy, n_gz, traces_ref, owner_ref, cell_ref, out_ref):
    me = lax.axis_index("gx")
    chunks = owner_ref.shape[0]
    owner_ids = iota((n_gy, 128), 0)
    picks = []
    for c in range(chunks):
        owner = owner_ref[c : c + 1, :]
        local = owner - me * (n_gy * n_gz)
        dest = lax.shift_right_arithmetic(local, n_gz.bit_length() - 1)
        picks.append(jnp.where(owner_ids == dest, 1.0, 0.0).astype(F32))
    all_picks = jnp.concatenate(picks, axis=0)
    before = (iota((128, 128), 0) < iota((128, 128), 1)).astype(F32).astype(BF16)
    prefix = jnp.dot(all_picks.astype(BF16), before, preferred_element_type=F32)
    offset = jnp.zeros((n_gy, 1), F32)
    slot_ids = iota((128, 128), 0)
    slots_low, slots_high, left, right = [], [], [], []
    for c in range(chunks):
        pick = picks[c]
        rank = jnp.sum(pick * (prefix[c * n_gy : (c + 1) * n_gy] + offset), axis=0, keepdims=True)
        offset = offset + jnp.sum(pick, axis=1, keepdims=True)
        rank = rank.astype(jnp.int32)
        slots_low.append(jnp.where(slot_ids == rank, 1.0, 0.0).astype(BF16))
        slots_high.append(jnp.where(slot_ids == rank + CAP, 1.0, 0.0).astype(BF16))
        first = traces_ref[0:1, c * 128 : (c + 1) * 128]
        second = traces_ref[1:2, c * 128 : (c + 1) * 128]
        cell = cell_ref[c : c + 1, :].astype(F32)
        left.append(
            jnp.concatenate([pick * s for s in split3(first) + split3(cell)], axis=0).astype(BF16)
        )
        right.append(jnp.concatenate([pick * s for s in split3(second)], axis=0).astype(BF16))
    low = jnp.concatenate(slots_low, axis=1)
    high = jnp.concatenate(slots_high, axis=1)
    left = lax.dot_general(jnp.concatenate(left, axis=1), low, NT, preferred_element_type=F32)
    right = lax.dot_general(jnp.concatenate(right, axis=1), high, NT, preferred_element_type=F32)

    def joined(value, at):
        parts = [value[(at + i) * n_gy : (at + i + 1) * n_gy] for i in range(3)]
        return parts[0] + parts[1] + parts[2]

    values = joined(left, 0) + joined(right, 0)
    cells = joined(left, 3)
    out_ref[...] = jnp.zeros_like(out_ref)
    for d in range(n_gy):
        out_ref[d, 0:1, :] = values[d : d + 1, :]
        out_ref[d, 1:2, :] = cells[d : d + 1, :]


def store_y_faces(src_ref, low_ref, high_ref):
    cx, cy, _ = src_ref.shape
    half = cx // 2
    for x in range(half):
        one, two = src_ref[x], src_ref[x + half]
        low_ref[x] = jnp.concatenate([one[0:4], two[0:4]], axis=0)
        high_ref[x] = jnp.concatenate([one[cy - 4 : cy], two[cy - 4 : cy]], axis=0)


def x_faces(ref):
    cx = ref.shape[0]
    return ref.at[0:4], ref.at[cx - 4 : cx]


def at_edges(axis):
    at = lax.axis_index(axis)
    return at == 0, at == lax.axis_size(axis) - 1


class Copier:
    def __init__(self, sems):
        self.sems, self.used, self.open = sems, 0, []

    def start(self, src, dst):
        copy = pltpu.make_async_copy(src, dst, self.sems.at[self.used])
        self.used += 1
        copy.start()
        return copy

    def send(self, src, dst):
        self.open.append(self.start(src, dst))

    def close(self):
        for copy in self.open:
            copy.wait()


def depth_rows(cx, cy):
    return -(-cx * cy // 128) * 8


def depth_faces(src_ref, out_ref):
    cx, cy, _ = src_ref.shape
    per = cy // 8
    group = lax.shift_right_logical(iota((8, 128), 1), 3)
    for begin in range(0, cx * per, 16):
        packed = jnp.zeros((8, 128), F32)
        for i in range(begin, min(begin + 16, cx * per)):
            k = i - begin
            row = src_ref[i // per, i % per * 8 : i % per * 8 + 8, :]
            packed = jnp.where(group == k, pltpu.roll(row, 4 + 8 * k, 1), packed)
        out_ref[begin // 2 : begin // 2 + 8, :] = packed


def send_kernel(
    n_gy, n_gz, traces_hbm, owner_hbm, cell_hbm, now_hbm,
    packed_hbm, x0_hbm, x1_hbm, y0_hbm, y1_hbm, z_hbm,
    traces_ref, owner_ref, cell_ref, now_ref, packed_ref, y0_ref, y1_ref, z_ref, sems,
):
    cx, cy, cz = now_ref.shape
    copier = Copier(sems)
    pairs = ((traces_hbm, traces_ref), (owner_hbm, owner_ref), (cell_hbm, cell_ref))
    records = [copier.start(src, dst) for src, dst in pairs]
    now = copier.start(now_hbm, now_ref)
    for copy in records:
        copy.wait()
    pack_records(n_gy, n_gz, traces_ref, owner_ref, cell_ref, packed_ref)
    copier.send(packed_ref, packed_hbm)
    now.wait()
    for src, dst in zip(x_faces(now_ref), (x0_hbm, x1_hbm)):
        copier.send(src, dst)
    store_y_faces(now_ref, y0_ref, y1_ref)
    copier.send(y0_ref, y0_hbm)
    copier.send(y1_ref, y1_hbm)
    depth_faces(now_ref, z_ref)
    copier.send(z_ref, z_hbm)
    copier.close()


def bin_records(recv_ref, cx, cy, cz):
    senders = recv_ref.shape[0]
    half = senders // 2
    values = recv_ref[:, 0, :]
    cells = recv_ref[:, 1, :]
    low = iota((half, 128), 1) < CAP
    rolled = pltpu.roll(values, CAP, 1)
    first = jnp.where(low, values[:half], rolled[half:])
    second = jnp.where(low, rolled[:half], values[half:])
    cell = jnp.where(low, cells[:half], pltpu.roll(cells, CAP, 1)[half:]).astype(jnp.int32)
    depth = lax.bitwise_and(cell, cz - 1)
    plane = lax.shift_right_logical(cell, cz.bit_length() - 1)
    at_x = plane // cy
    at_y = plane - at_x * cy
    column = at_x * SURF + depth
    columns = -(-cx * SURF // 128) * 128
    pieces = split3(first) + split3(second)
    row_ids = iota((cy, 128), 0)
    column_ids = iota((columns, 128), 0)
    total = None
    step = 4
    for begin in range(0, half, step):
        lefts, rights = [], []
        for s in range(begin, begin + step):
            hit = row_ids == at_y[s : s + 1]
            lefts.append(
                jnp.concatenate([jnp.where(hit, p[s : s + 1], 0.0) for p in pieces], axis=0).astype(BF16)
            )
            rights.append(jnp.where(column_ids == column[s : s + 1], 1.0, 0.0).astype(BF16))
        term = lax.dot_general(
            jnp.concatenate(lefts, axis=1), jnp.concatenate(rights, axis=1), NT,
            preferred_element_type=F32,
        )
        total = term if total is None else total + term
    part = [total[i * cy : (i + 1) * cy] for i in range(6)]
    return part[0] + part[1] + part[2], part[3] + part[4] + part[5]


def start_halo(copier, pad_ref, halo_hbm, halo_refs):
    cx, cy = pad_ref.shape[0] - 8, pad_ref.shape[1] - 16
    places = (pad_ref.at[0:4, 8 : 8 + cy, :], pad_ref.at[4 + cx : 8 + cx, 8 : 8 + cy, :])
    return [copier.start(src, dst) for src, dst in zip(halo_hbm, places + tuple(halo_refs))]


def fill_xy(pad_ref, before_ref, after_ref):
    cx, cy, cz = pad_ref.shape[0] - 8, pad_ref.shape[1] - 16, pad_ref.shape[2]
    half = cx // 2
    for edge, begin in zip(at_edges("gx"), (0, 4 + cx)):

        @pl.when(edge)
        def _(begin=begin):
            pad_ref[begin : begin + 4, 8 : 8 + cy, :] = jnp.zeros((4, cy, cz), F32)

    first, last = at_edges("gy")
    for x in range(half):
        before = jnp.where(first, 0.0, before_ref[x])
        after = jnp.where(last, 0.0, after_ref[x])
        pad_ref[4 + x, 4:8, :] = before[0:4]
        pad_ref[4 + half + x, 4:8, :] = before[4:8]
        pad_ref[4 + x, 8 + cy : 12 + cy, :] = after[0:4]
        pad_ref[4 + half + x, 8 + cy : 12 + cy, :] = after[4:8]


def depth_correction(own_ref, before_ref, after_ref, out_ref):
    own = own_ref[...]
    cell = lax.bitwise_and(iota(own.shape, 1), 7)
    first, last = at_edges("gz")
    before, after = jnp.where(first, 0.0, before_ref[...]), jnp.where(last, 0.0, after_ref[...])
    high, middle, low = split3(jnp.where(cell < 4, before, after) - own)
    source, target = iota((128, 128), 0), iota((128, 128), 1)
    near = lax.shift_right_logical(source, 3) == lax.shift_right_logical(target, 3)
    near = near & (lax.bitwise_and(source, 4) != lax.bitwise_and(target, 4))
    distance = jnp.where(near, jnp.abs(source - target), 0)
    weight = jnp.zeros((128, 128), F32)
    for j in range(1, 5):
        weight = jnp.where(distance == j, COEFFS[j], weight)
    w = split3(weight)
    left = jnp.concatenate([high, middle, low, high, middle, high], axis=1).astype(BF16)
    right = jnp.concatenate([w[0], w[0], w[0], w[1], w[1], w[2]], axis=0).astype(BF16)
    result = jnp.dot(left, right, preferred_element_type=F32)
    lane = iota((8, 128), 1)
    outer = (lane < 4) | (lane >= 124)
    for i in range(out_ref.shape[0]):
        row = result[i // 16 * 8 : i // 16 * 8 + 8]
        out_ref[i] = jnp.where(outer, pltpu.roll(row, 124 - i % 16 * 8, 1), 0.0)


def depth_weights():
    apart = jnp.abs(iota((128, 128), 0) - iota((128, 128), 1))
    apart = jnp.minimum(apart, 128 - apart)
    weight = jnp.zeros((128, 128), F32)
    for j in range(1, 5):
        weight = jnp.where(apart == j, COEFFS[j], weight)
    high, middle, _ = split3(weight)
    return jnp.concatenate([high, high, middle], axis=0).astype(BF16)


def depth_part(pad_ref, weights, begin, cy, zc_ref):
    rows = CHUNK * cy
    value = pad_ref[4 + begin : 4 + begin + CHUNK, 8 : 8 + cy, :].reshape(rows, 128)
    high, middle, _ = split3(value)
    left = jnp.concatenate([high, middle, high], axis=1).astype(BF16)
    result = jnp.dot(left, weights, preferred_element_type=F32)
    at = begin * cy // 8
    zc_ref[at : at + rows // 8] = zc_ref[at : at + rows // 8] + result.reshape(rows // 8, 8, 128)


def lap_at(pad_ref, zc_ref, x, cy):
    center = pad_ref[x + 4, 8 : 8 + cy, :]
    per = cy // 8
    total = (3.0 * COEFFS[0]) * center + zc_ref[x * per : (x + 1) * per].reshape(cy, center.shape[1])
    for j in range(1, 5):
        pair = pad_ref[x + 4 - j, 8 : 8 + cy, :] + pad_ref[x + 4 + j, 8 : 8 + cy, :]
        pair = pair + (pad_ref[x + 4, 8 - j : 8 - j + cy, :] + pad_ref[x + 4, 8 + j : 8 + j + cy, :])
        total = total + COEFFS[j] * pair
    return center, total


def spread_sources(sources, out_ref):
    for group in range(out_ref.shape[0]):
        out_ref[group] = sources[:, group * 128 : (group + 1) * 128]


def source_at(source_ref, x, low):
    piece = source_ref[x // 16]
    if x % 16:
        piece = pltpu.roll(piece, 128 - x % 16 * SURF, 1)
    return jnp.where(low, piece, 0.0)


def center_copy(copier, hbm, pad_ref):
    cx, cy = pad_ref.shape[0] - 8, pad_ref.shape[1] - 16
    return copier.start(hbm, pad_ref.at[4 : 4 + cx, 8 : 8 + cy, :])


def start_chunks(copier, pairs, cx):
    chunks = []
    for begin in range(0, cx, CHUNK):
        part = pl.ds(begin, CHUNK)
        chunks.append([copier.start(src.at[part], dst.at[part]) for src, dst in pairs])
    return chunks


def first_kernel(
    recv_hbm, x0_hbm, x1_hbm, y0_hbm, y1_hbm, z_hbm, z0_hbm, z1_hbm,
    now_hbm, late_hbm, courant_hbm,
    fresh_hbm, source_hbm, xs0_hbm, xs1_hbm, ys0_hbm, ys1_hbm, zs_hbm,
    recv_ref, pad_ref, y0_ref, y1_ref, z_ref, z0_ref, z1_ref, zc_ref, late_ref, courant_ref,
    fresh_ref, source_ref, later_ref, ys0_ref, ys1_ref, zs_ref, sems,
):
    cx, cy, cz = fresh_ref.shape
    copier = Copier(sems)
    recv = copier.start(recv_hbm, recv_ref)
    halo = start_halo(
        copier, pad_ref, (x0_hbm, x1_hbm, y0_hbm, y1_hbm, z_hbm, z0_hbm, z1_hbm),
        (y0_ref, y1_ref, z_ref, z0_ref, z1_ref),
    )
    now = center_copy(copier, now_hbm, pad_ref)
    chunks = start_chunks(copier, ((late_hbm, late_ref), (courant_hbm, courant_ref)), cx)
    recv.wait()
    sources, later = bin_records(recv_ref, cx, cy, cz)
    spread_sources(sources, source_ref)
    spread_sources(later, later_ref)
    copier.send(later_ref, source_hbm)
    for copy in halo:
        copy.wait()
    fill_xy(pad_ref, y0_ref, y1_ref)
    depth_correction(z_ref, z0_ref, z1_ref, zc_ref)
    now.wait()
    low = iota((cy, cz), 1) < SURF
    weights = depth_weights()

    def step(x):
        center, lap = lap_at(pad_ref, zc_ref, x, cy)
        lap = lap + source_at(source_ref, x, low)
        fresh_ref[x] = 2.0 * center - late_ref[x] + courant_ref[x] * lap

    for c, copies in enumerate(chunks):
        for copy in copies:
            copy.wait()
        part = pl.ds(c * CHUNK, CHUNK)
        depth_part(pad_ref, weights, c * CHUNK, cy, zc_ref)
        for x in range(c * CHUNK, (c + 1) * CHUNK):
            step(x)
        copier.send(fresh_ref.at[part], fresh_hbm.at[part])
    for src, dst in zip(x_faces(fresh_ref), (xs0_hbm, xs1_hbm)):
        copier.send(src, dst)
    store_y_faces(fresh_ref, ys0_ref, ys1_ref)
    copier.send(ys0_ref, ys0_hbm)
    copier.send(ys1_ref, ys1_hbm)
    depth_faces(fresh_ref, zs_ref)
    copier.send(zs_ref, zs_hbm)
    copier.close()


def second_kernel(
    now_hbm, source_hbm, x0_hbm, x1_hbm, y0_hbm, y1_hbm, z_hbm, z0_hbm, z1_hbm,
    late_hbm, courant_hbm, forward_hbm, image_hbm,
    fresh_hbm, image_out_hbm,
    source_ref, pad_ref, y0_ref, y1_ref, z_ref, z0_ref, z1_ref, zc_ref, late_ref, courant_ref,
    forward0_ref, forward1_ref, image_ref, fresh_ref, sems,
):
    cx, cy, cz = fresh_ref.shape
    copier = Copier(sems)
    halo = start_halo(
        copier, pad_ref, (x0_hbm, x1_hbm, y0_hbm, y1_hbm, z_hbm, z0_hbm, z1_hbm),
        (y0_ref, y1_ref, z_ref, z0_ref, z1_ref),
    )
    now = center_copy(copier, now_hbm, pad_ref)
    source = copier.start(source_hbm, source_ref)
    chunks = start_chunks(
        copier,
        (
            (late_hbm, late_ref), (courant_hbm, courant_ref), (image_hbm, image_ref),
            (forward_hbm.at[0], forward0_ref), (forward_hbm.at[1], forward1_ref),
        ),
        cx,
    )
    for copy in halo:
        copy.wait()
    fill_xy(pad_ref, y0_ref, y1_ref)
    depth_correction(z_ref, z0_ref, z1_ref, zc_ref)
    now.wait()
    source.wait()
    low = iota((cy, cz), 1) < SURF
    weights = depth_weights()

    def step(x):
        center, lap = lap_at(pad_ref, zc_ref, x, cy)
        lap = lap + source_at(source_ref, x, low)
        fresh = 2.0 * center - late_ref[x] + courant_ref[x] * lap
        fresh_ref[x] = fresh
        image = image_ref[x] + forward0_ref[x].astype(F32) * center
        image_ref[x] = image + forward1_ref[x].astype(F32) * fresh

    for c, copies in enumerate(chunks):
        for copy in copies:
            copy.wait()
        part = pl.ds(c * CHUNK, CHUNK)
        depth_part(pad_ref, weights, c * CHUNK, cy, zc_ref)
        for x in range(c * CHUNK, (c + 1) * CHUNK):
            step(x)
        copier.send(fresh_ref.at[part], fresh_hbm.at[part])
        copier.send(image_ref.at[part], image_out_hbm.at[part])
    copier.close()


def turn(value, axis, by):
    count = lax.axis_size(axis)
    return lax.ppermute(value, axis, [(i, (i + by) % count) for i in range(count)])


def exchange(x_low, x_high, y_low, y_high, z, both):
    z_before, z_after = turn(z, "gz", 1), turn(z, "gz", -1)
    y_before, y_after = turn(y_high, "gy", 1), turn(y_low, "gy", -1)
    x_before = turn(x_high, "gx", 1)
    if both:
        x_low, z_before, z_after = lax.optimization_barrier((x_low, z_before, z_after))
    else:
        x_low, z_after = lax.optimization_barrier((x_low, z_after))
    x_after = turn(x_low, "gx", -1)
    return x_before, x_after, y_before, y_after, z, z_before, z_after


def struct(*shape):
    return jax.ShapeDtypeStruct(shape, F32)


def vm(*shape, dtype=F32):
    return pltpu.VMEM(shape, dtype)


def call(kernel, outs, args, scratch, copies):
    anywhere = pl.BlockSpec(memory_space=pl.ANY)
    size = sum(a.size * a.dtype.itemsize for a in args) + sum(o.size * 4 for o in outs)
    return pl.pallas_call(
        kernel,
        out_shape=outs,
        in_specs=[anywhere] * len(args),
        out_specs=[anywhere] * len(outs),
        scratch_shapes=list(scratch) + [pltpu.SemaphoreType.DMA((copies,))],
        compiler_params=pltpu.CompilerParams(vmem_limit_bytes=63_480_000),
        cost_estimate=pl.CostEstimate(flops=10**10, bytes_accessed=size, transcendentals=0),
    )(*args)


def on_device(adjoint_now, adjoint_late, courant, forward, image_in, traces, rec_owner, rec_cell):
    cx, cy, cz = adjoint_now.shape
    n_gy, n_gz = lax.axis_size("gy"), lax.axis_size("gz")
    chunks = rec_owner.shape[0] // 128
    groups = -(-cx * SURF // 128)
    block = struct(cx, cy, cz)
    x_face, y_face = struct(4, cy, cz), struct(cx // 2, 8, cz)
    faces = (x_face, x_face, y_face, y_face, struct(depth_rows(cx, cy), 128))
    grid, y_in, z_in = vm(cx, cy, cz), vm(cx // 2, 8, cz), vm(depth_rows(cx, cy), 128)
    pad = vm(cx + 8, cy + 16, cz)
    corrections = vm(cx * cy // 8, 8, cz)
    slots = (n_gy * n_gz, 2, 128)
    packed, *out_faces = call(
        functools.partial(send_kernel, n_gy, n_gz), (struct(*slots),) + faces,
        (traces, rec_owner.reshape(chunks, 128), rec_cell.reshape(chunks, 128), adjoint_now),
        (
            vm(*traces.shape), vm(chunks, 128, dtype=jnp.int32), vm(chunks, 128, dtype=jnp.int32),
            grid, vm(*slots), y_in, y_in, z_in,
        ),
        10,
    )
    received = lax.all_to_all(packed, ("gz", "gy"), 0, 0)
    halo = exchange(*out_faces, False)
    turns = cx // CHUNK
    source = (groups, cy, 128)
    middle, later, *out_faces = call(
        first_kernel, (block, struct(*source)) + faces,
        (received,) + halo + (adjoint_now, adjoint_late, courant),
        (
            vm(*slots), pad, y_in, y_in, z_in, z_in, z_in, corrections, grid, grid,
            grid, vm(*source), vm(*source), y_in, y_in, z_in,
        ),
        15 + 3 * turns,
    )
    halo = exchange(*out_faces, True)
    half = vm(cx, cy, cz, dtype=BF16)
    newest, image = call(
        second_kernel, (block, block),
        (middle, later) + halo + (adjoint_now, courant, forward, image_in),
        (
            vm(*source), pad, y_in, y_in, z_in, z_in, z_in, corrections, grid, grid,
            half, half, grid, grid,
        ),
        9 + 7 * turns,
    )
    return newest, middle, image


def solution(mesh):
    grid = P("gx", "gy", "gz")
    return jax.shard_map(
        on_device,
        mesh=mesh,
        in_specs=(
            grid, grid, grid, P(None, "gx", "gy", "gz"), grid,
            P(None, ("gy", "gz")), P(("gy", "gz")), P(("gy", "gz")),
        ),
        out_specs=(grid, grid, grid),
        check_vma=False,
    )
```
